256 devices in a mesh: row: 8 (over z), col: 32 (over x, y, core).
Axes of the slice: x: 4, y: 4, z: 8, core: 2. Of those that a mesh axis runs over, the one named last changes fastest.
Arguments:
- trailing: float32 [32768, 12288], P('row', 'col'), may hold values from -6 to 6
- leaf_vectors: float32 [32768, 256], P(('row', 'col')), may hold values from -1 to 1, as said below
- leaf_factor: float32 [2048, 256], P(('row', 'col')), may hold values from -1 to 2, as said below
- tree_vectors: float32 [2048, 256], P(('row', 'col')), may hold values from -1 to 1, as said below
- tree_factor: float32 [2048, 256], P(('row', 'col')), may hold values from -1 to 2, as said below
Outputs:
- updated: float32 [32768, 12288], P('row', 'col')
The draws below stay inside these ranges and needn't reach their ends.
Inputs may be any that keep to these rules, and one draw needn't show every extreme that they name: `leaf_vectors`: in each row block of 4096 rows, row r < 256 of the block holds 1 in column r and 0 in every column after r. `leaf_factor`: each 256 x 256 block is upper triangular with its diagonal between 1 and 2. `tree_vectors`: each 256 x 256 block is upper triangular. `tree_factor`: each 256 x 256 block is upper triangular with its diagonal between 1 and 2.
All inputs are finite; a program needn't handle non-finite values.
Results may differ from the reference program's by a relative error of at most 0.0002.
Values sent between devices are 32-bit elements; how exact they have to be, the bound alone decides.
A program may use at most 128 MiB of HBM per device.

```python
import math
import jax
import jax.numpy as jnp
from jax import lax

B = 256
R_DEV = 4096
M = 32768
N = 12288


def draw_leaf_vectors(key, part):
    sampled = jax.random.truncated_normal(jax.random.fold_in(key, 11), -6.0, 6.0, (M, B), jnp.float32) * (1.0 / math.sqrt(R_DEV))
    row_in_block = (jnp.arange(M) % R_DEV)[:, None]
    column_ids = jnp.arange(B)[None, :]
    return jnp.where(column_ids < row_in_block, sampled, jnp.where(column_ids == row_in_block, 1.0, 0.0)).astype(jnp.float32)


def triangular_factor(key, salt):
    count = M // R_DEV * B
    folded = jax.random.fold_in(key, salt)
    diagonal_values = jax.random.uniform(jax.random.fold_in(folded, 1), (count, B), jnp.float32, 1.0, 2.0)
    sampled = jax.random.truncated_normal(jax.random.fold_in(folded, 2), -4.0, 4.0, (count, B), jnp.float32) * (0.5 / math.sqrt(B))
    row_in_block = (jnp.arange(count) % B)[:, None]
    column_ids = jnp.arange(B)[None, :]
    return jnp.where(column_ids > row_in_block, sampled, jnp.where(column_ids == row_in_block, diagonal_values, 0.0)).astype(jnp.float32)


def draw_leaf_factor(key, part):
    return triangular_factor(key, 21)


def draw_tree_factor(key, part):
    return triangular_factor(key, 23)


def draw_tree_vectors(key, part):
    count = M // R_DEV * B
    sampled = jax.random.truncated_normal(jax.random.fold_in(key, 31), -4.0, 4.0, (count, B), jnp.float32) * (1.0 / math.sqrt(B))
    row_in_block = (jnp.arange(count) % B)[:, None]
    column_ids = jnp.arange(B)[None, :]
    return jnp.where(column_ids >= row_in_block, sampled, 0.0).astype(jnp.float32)


def shard_levels(stream_key, dims, shards, low, largest):
    gain = 1.0
    for position, shards_of in shards:
        steps = jax.random.uniform(jax.random.fold_in(jax.random.fold_in(stream_key, 6), position), (shards_of,), jnp.float32, low / len(shards), largest / len(shards))
        gain = gain * jnp.repeat(jnp.exp(steps), dims[position] // shards_of).reshape((-1,) + (1,) * (len(dims) - 1 - position))
    return gain


def gaussian(stream_key, extent, scale, most, split=(), held_as=jnp.bfloat16):
    result = scale * jax.random.normal(stream_key, extent, jnp.float32)
    if split:
        result = result * shard_levels(stream_key, extent, split, -0.22, 0.18)
    return jnp.clip(result, -most, most).astype(held_as)


def setup_inputs(seed: int = 0) -> dict:
    key_of = jax.random.split(jax.random.key(seed), 6)
    trailing = gaussian(key_of[0], (M, N), 1.0, 6.0, ((0, 8), (1, 32)), jnp.float32)
    leaf_vectors = draw_leaf_vectors(jax.random.fold_in(key_of[5], 71), 0)
    leaf_factor = draw_leaf_factor(jax.random.fold_in(key_of[5], 71), 0)
    tree_vectors = draw_tree_vectors(jax.random.fold_in(key_of[5], 71), 0)
    tree_factor = draw_tree_factor(jax.random.fold_in(key_of[5], 71), 0)
    return dict(trailing=trailing, leaf_vectors=leaf_vectors, leaf_factor=leaf_factor, tree_vectors=tree_vectors, tree_factor=tree_factor)


highest = lax.Precision.HIGHEST
contract_rows = (((0,), (0,)), ((), ()))


def left_product(first, second):
    return lax.dot_general(first, second, contract_rows, precision=highest, preferred_element_type=jnp.float32)


def plain_product(first, second):
    return jnp.dot(first, second, precision=highest, preferred_element_type=jnp.float32)


def apply_leaf(operands):
    row_block, vectors, factor = operands
    weights = left_product(factor, left_product(vectors, row_block))
    return row_block - plain_product(vectors, weights)


def reference(trailing, leaf_vectors, leaf_factor, tree_vectors, tree_factor):
    blocks_count = trailing.shape[0] // R_DEV
    blocks = trailing.reshape(blocks_count, R_DEV, trailing.shape[1])
    updated = lax.map(apply_leaf, (blocks, leaf_vectors.reshape(blocks_count, R_DEV, B), leaf_factor.reshape(blocks_count, B, B)))
    top_rows = [updated[block_index, :B, :] for block_index in range(blocks_count)]
    stride = 1
    while stride < blocks_count:
        for leader in range(0, blocks_count, 2 * stride):
            partner = leader + stride
            vectors = tree_vectors[partner * B:(partner + 1) * B]
            factor = tree_factor[partner * B:(partner + 1) * B]
            weights = left_product(factor, top_rows[leader] + left_product(vectors, top_rows[partner]))
            top_rows[leader] = top_rows[leader] - weights
            top_rows[partner] = top_rows[partner] - plain_product(vectors, weights)
        stride = stride * 2
    return updated.at[:, :B, :].set(jnp.stack(top_rows)).reshape(trailing.shape)
```

```python
import jax
import jax.numpy as jnp
from jax import lax
from jax.experimental import pallas as pl
from jax.experimental.pallas import tpu as pltpu
from jax.sharding import PartitionSpec as P

MESH = pl.DeviceIdType.MESH
HIGH = lax.Precision.HIGH
F32 = jnp.float32

PANEL = 256
ROWS = 4096
COLS = 384
CHUNK = 128
CHUNKS = COLS // CHUNK
SIDE = 4
CHIPS = 16
DEVS = 32

BLOCK = 168
OWN_U, OWN_F = 64, 72
SECOND = 80
S_ROW = 144
FOREIGN = 152
STREAMS = ((0, 80, 40, 0), (SECOND, 72, 40, 1), (FOREIGN, 16, 8, 1))

CLASSES = (
    ((1, 0), (3, 0), (0, 1), (0, 3)),
    ((2, 0), (0, 2)),
    ((1, 1), (1, 3), (3, 1), (3, 3)),
    ((1, 2), (3, 2), (2, 1), (2, 3)),
    ((2, 2),),
)


def pick(index, values):
    result = jnp.int32(values[-1])
    for k in range(len(values) - 2, -1, -1):
        result = jnp.where(index == k, jnp.int32(values[k]), result)
    return result


def dot(a, b):
    return jnp.dot(a, b, precision=HIGH, preferred_element_type=F32)


def dot_t(a, b):
    return lax.dot_general(a, b, (((0,), (0,)), ((), ())), precision=HIGH, preferred_element_type=F32)


def kernel(
    c_hbm, v_hbm, s_hbm, u_hbm, f_hbm, out_hbm,
    buf, cbuf, zacc, wacc, xown, pair, leads, xfin, fac_u, fac_ut, fac_ft,
    load_sem, c_sem, send_sem, recv_sem, half_sem, sib_sem, sib2_sem, uf_send, uf_recv,
    a_send, a_recv, b_send, b_recv, l_send, l_recv, out_sem, top_sem,
):
    z = lax.axis_index("row")
    col = lax.axis_index("col")
    core = lax.rem(col, 2)
    chip = lax.div(col, 2)
    x = lax.div(chip, SIDE)
    y = lax.rem(chip, SIDE)
    role = lax.rem(z, 4)
    group = lax.div(z, 4)
    sibling = col + 1 - 2 * core

    def chip_at(dx, dy):
        return lax.rem(x + dx, SIDE) * SIDE + lax.rem(y + dy, SIDE)

    def neighbour(axis, step):
        return chip_at(step, 0) * 2 + core if axis == 0 else chip_at(0, step) * 2 + core

    loads = [
        pltpu.make_async_copy(v_hbm.at[pl.ds(0, 64)], buf.at[col, pl.ds(0, 64)], load_sem.at[0]),
        pltpu.make_async_copy(v_hbm.at[pl.ds(64, 64)], buf.at[col, pl.ds(SECOND, 64)], load_sem.at[1]),
        pltpu.make_async_copy(s_hbm, buf.at[col, pl.ds(S_ROW, 8)], load_sem.at[2]),
        pltpu.make_async_copy(u_hbm, buf.at[col, pl.ds(OWN_U, 8)], load_sem.at[3]),
        pltpu.make_async_copy(f_hbm, buf.at[col, pl.ds(OWN_F, 8)], load_sem.at[4]),
    ]
    for load in loads:
        load.start()
    load_c = pltpu.make_async_copy(c_hbm, cbuf, c_sem)
    load_c.start()

    barrier = pltpu.get_barrier_semaphore()
    for axis in (0, 1):
        for step in (1, 3):
            pl.semaphore_signal(barrier, inc=1, device_id=(z, neighbour(axis, step)), device_id_type=MESH)
    pl.semaphore_signal(barrier, inc=1, device_id=(z, sibling), device_id_type=MESH)
    for step in range(1, 8):
        pl.semaphore_signal(barrier, inc=1, device_id=(lax.rem(z + step, 8), col), device_id_type=MESH)
    pl.semaphore_wait(barrier, 12)
    for load in loads:
        load.wait()

    uf_to = pick(z, (3, 4, 1, 2, 0, 7, 5, 6))
    uf_copy = pltpu.make_async_remote_copy(
        src_ref=buf.at[col, pl.ds(OWN_U, 16)], dst_ref=buf.at[col, pl.ds(FOREIGN, 16)],
        send_sem=uf_send, recv_sem=uf_recv, device_id=(uf_to, col), device_id_type=MESH,
    )
    uf_copy.start()

    def send(block, start, rows, to, sem):
        pltpu.make_async_remote_copy(
            src_ref=buf.at[block, pl.ds(start, rows)], dst_ref=buf.at[block, pl.ds(start, rows)],
            send_sem=send_sem, recv_sem=sem, device_id=(z, to), device_id_type=MESH,
        ).start()

    def arrived(block, start, rows, sem):
        pltpu.make_async_copy(buf.at[block, pl.ds(start, rows)], buf.at[block, pl.ds(start, rows)], sem).wait()

    def offset_index(axis, i, j):
        i, j = i % SIDE, j % SIDE
        return (i * SIDE + j) if axis == 0 else (j * SIDE + i)

    def handle(h, dx, dy):
        start, rows, front, axis = STREAMS[h]
        i, j = (dx, dy) if axis == 0 else (dy, dx)
        block = chip_at(dx, dy) * 2 + core
        here = offset_index(axis, i, j)
        other = 1 - axis
        if (i, j) != (0, 0):
            if j == 2 or (j == 0 and i == 2):
                arrived(block, start, front, recv_sem.at[h, here])
                arrived(block, start + front, rows - front, half_sem.at[h, here])
            else:
                arrived(block, start, rows, recv_sem.at[h, here])
        if j == 0:
            if i == 0:
                send(block, start, rows, neighbour(axis, 1), recv_sem.at[h, offset_index(axis, 3, 0)])
                send(block, start, rows, neighbour(axis, 3), recv_sem.at[h, offset_index(axis, 1, 0)])
            elif i == 3:
                send(block, start, front, neighbour(axis, 1), recv_sem.at[h, offset_index(axis, 2, 0)])
            elif i == 1:
                send(block, start + front, rows - front, neighbour(axis, 3), half_sem.at[h, offset_index(axis, 2, 0)])
            send(block, start, rows, neighbour(other, 1), recv_sem.at[h, offset_index(axis, i, 3)])
            send(block, start, rows, neighbour(other, 3), recv_sem.at[h, offset_index(axis, i, 1)])
        elif j == 3:
            send(block, start, front, neighbour(other, 1), recv_sem.at[h, offset_index(axis, i, 2)])
        elif j == 1:
            send(block, start + front, rows - front, neighbour(other, 3), half_sem.at[h, offset_index(axis, i, 2)])
        send(block, start, rows, sibling, sib2_sem if h == 2 else sib_sem.at[h, here])

    def vectors(q):
        parts = []
        for k in (0, 1):
            parts += [buf[2 * q + k, pl.ds(0, 64), :], buf[2 * q + k, pl.ds(SECOND, 64), :]]
        return jnp.concatenate(parts, axis=0)

    def project(chips):
        @pl.loop(0, len(chips))
        def _(t):
            dx = pick(t, [c[0] for c in chips])
            dy = pick(t, [c[1] for c in chips])
            q = chip_at(dx, dy)
            block = 2 * q + 1 - core
            for h in (0, 1):
                arrived(block, STREAMS[h][0], STREAMS[h][1], sib_sem.at[h, dx * SIDE + dy])
            rows = pl.ds(pl.multiple_of(q * 256, 256), 256)
            zacc[...] += dot_t(vectors(q), cbuf[rows, :])

    handle(0, 0, 0)
    handle(1, 0, 0)
    zacc[...] = jnp.zeros_like(zacc)
    load_c.wait()
    uf_copy.wait()
    ready = ((0, 0),)
    for n, chips in enumerate(CLASSES):
        for h in (0, 1):
            for dx, dy in chips:
                handle(h, dx, dy)
        for dx, dy in (CLASSES[n - 1] if n else ((0, 0),)):
            handle(2, dx, dy)
        if n:
            project(ready + CLASSES[0] if n == 1 else CLASSES[n - 1])
    handle(2, 2, 2)
    project(CLASSES[-1])

    factor = buf[:, pl.ds(S_ROW, 8), :].reshape(PANEL, PANEL)
    wacc[...] = dot_t(factor, zacc[...])
    top = cbuf[pl.ds(0, PANEL), :] - dot(vectors(jnp.int32(0)), wacc[...])
    for c in range(CHUNKS):
        xown[c] = top[:, c * CHUNK : (c + 1) * CHUNK]

    def a_copy(c):
        to = jnp.where(role == 3, z - 1, z + 1)
        return pltpu.make_async_remote_copy(
            src_ref=xown.at[c], dst_ref=pair.at[0, c], send_sem=a_send.at[c], recv_sem=a_recv.at[c],
            device_id=(to, col), device_id_type=MESH,
        )

    def b_copy(c):
        to = jnp.where(role == 1, z + 1, z - 1)
        return pltpu.make_async_remote_copy(
            src_ref=pair.at[1, c], dst_ref=pair.at[2, c], send_sem=b_send.at[c], recv_sem=b_recv.at[c],
            device_id=(to, col), device_id_type=MESH,
        )

    def l_copy(c):
        to = jnp.where(role == 1, z - 1, lax.rem(z + 2, 8))
        return pltpu.make_async_remote_copy(
            src_ref=leads.at[2, c], dst_ref=leads.at[group, c], send_sem=l_send.at[c],
            recv_sem=l_recv.at[group, c], device_id=(to, col), device_id_type=MESH,
        )

    @pl.when(role != 1)
    def _():
        for c in range(CHUNKS):
            a_copy(c).start()

    def lower(first, last):
        @pl.loop(first, last)
        def _(q):
            rows = pl.ds(pl.multiple_of(q * 256, 256), 256)
            cbuf[rows, :] = cbuf[rows, :] - dot(vectors(q), wacc[...])
            pltpu.make_async_copy(cbuf.at[rows], out_hbm.at[rows], out_sem).start()

    chain = (role == 1) | (role == 2)
    cut = jnp.where(chain, jnp.int32(5), jnp.int32(CHIPS))

    pltpu.make_async_copy(fac_u.at[0], fac_u.at[0], sib2_sem).wait()

    def prepare(slot, foreign):
        at = jnp.where(foreign, jnp.int32(FOREIGN), jnp.int32(OWN_U))
        at = pl.multiple_of(at, 8)
        u = buf[:, pl.ds(at, 8), :].reshape(PANEL, PANEL)
        f = buf[:, pl.ds(at + 8, 8), :].reshape(PANEL, PANEL)
        fac_u[slot] = u
        fac_ut[slot] = u.T
        fac_ft[slot] = f.T

    prepare(0, (role == 2) | (z == 0))
    prepare(1, role == 1)

    lower(1, cut)

    def weights(slot, leader, partner):
        return dot(fac_ft[slot], leader + dot(fac_ut[slot], partner))

    @pl.when(role != 0)
    def _():
        for c in range(CHUNKS):
            a_copy(c).wait_recv()
            own, got = xown[c], pair[0, c]
            leader = jnp.where(role == 2, own, got)
            partner = jnp.where(role == 2, got, own)
            w = weights(0, leader, partner)
            pair[1, c] = leader - w

            @pl.when(chain)
            def _():
                b_copy(c).start()

            @pl.when(role != 2)
            def _():
                xfin[c] = partner - dot(fac_u[0], w)

    @pl.when(chain)
    def _():
        for c in range(CHUNKS):
            b_copy(c).wait_recv()
            own, got = pair[1, c], pair[2, c]
            leader = jnp.where(role == 1, own, got)
            partner = jnp.where(role == 1, got, own)
            w = weights(1, leader, partner)
            leads[2, c] = leader - w
            l_copy(c).start()

            @pl.when(role == 2)
            def _():
                xfin[c] = partner - dot(fac_u[1], w)

    lower(cut, CHIPS)

    @pl.when(role == 0)
    def _():
        for c in range(CHUNKS):
            for k in (0, 1):
                pltpu.make_async_copy(leads.at[k, c], leads.at[k, c], l_recv.at[k, c]).wait()
            leader, partner = leads[0, c], leads[1, c]
            w = weights(0, leader, partner)

            @pl.when(z == 0)
            def _():
                xfin[c] = leader - w

            @pl.when(z != 0)
            def _():
                xfin[c] = partner - dot(fac_u[0], w)

    tops = [
        pltpu.make_async_copy(xfin.at[c], out_hbm.at[pl.ds(0, PANEL), pl.ds(c * CHUNK, CHUNK)], top_sem.at[c])
        for c in range(CHUNKS)
    ]
    for t in tops:
        t.start()

    pltpu.make_async_copy(buf.at[pl.ds(0, DEVS - 1)], buf.at[pl.ds(0, DEVS - 1)], send_sem).wait()

    @pl.when(role != 1)
    def _():
        for c in range(CHUNKS):
            a_copy(c).wait_send()

    @pl.when(chain)
    def _():
        for c in range(CHUNKS):
            b_copy(c).wait_send()
            l_copy(c).wait_send()

    lower_rows = pl.ds(PANEL, ROWS - PANEL)
    pltpu.make_async_copy(cbuf.at[lower_rows], out_hbm.at[lower_rows], out_sem).wait()
    for t in tops:
        t.wait()


def shards(trailing, leaf_vectors, leaf_factor, tree_vectors, tree_factor):
    dma = pltpu.SemaphoreType.DMA
    return pl.pallas_call(
        kernel,
        out_shape=jax.ShapeDtypeStruct((ROWS, COLS), F32),
        in_specs=[pl.BlockSpec(memory_space=pl.ANY)] * 5,
        out_specs=pl.BlockSpec(memory_space=pl.ANY),
        scratch_shapes=[
            pltpu.VMEM((DEVS, BLOCK, PANEL), F32),
            pltpu.VMEM((ROWS, COLS), F32),
            pltpu.VMEM((PANEL, COLS), F32),
            pltpu.VMEM((PANEL, COLS), F32),
            pltpu.VMEM((CHUNKS, PANEL, CHUNK), F32),
            pltpu.VMEM((3, CHUNKS, PANEL, CHUNK), F32),
            pltpu.VMEM((3, CHUNKS, PANEL, CHUNK), F32),
            pltpu.VMEM((CHUNKS, PANEL, CHUNK), F32),
            pltpu.VMEM((2, PANEL, PANEL), F32),
            pltpu.VMEM((2, PANEL, PANEL), F32),
            pltpu.VMEM((2, PANEL, PANEL), F32),
            dma((5,)), dma, dma, dma((3, CHIPS)), dma((3, CHIPS)), dma((2, CHIPS)), dma, dma, dma,
            dma((CHUNKS,)), dma((CHUNKS,)), dma((CHUNKS,)), dma((CHUNKS,)), dma((CHUNKS,)), dma((2, CHUNKS)),
            dma, dma((CHUNKS,)),
        ],
        compiler_params=pltpu.CompilerParams(
            collective_id=0, has_side_effects=True, vmem_limit_bytes=50 * 1024 * 1024
        ),
    )(trailing, leaf_vectors, leaf_factor, tree_vectors, tree_factor)


def solution(mesh):
    placed = (
        P("row", "col"),
        P(("row", "col"), None),
        P(("row", "col"), None),
        P(("row", "col"), None),
        P(("row", "col"), None),
    )
    return jax.shard_map(
        shards, mesh=mesh, in_specs=placed, out_specs=P("row", "col"), check_vma=False
    )
```

```python
import jax
import jax.numpy as jnp
from jax import lax
from jax.experimental import pallas as pl
from jax.experimental.pallas import tpu as pltpu
from jax.sharding import PartitionSpec as P

MESH = pl.DeviceIdType.MESH
HIGH = lax.Precision.HIGH
F32 = jnp.float32

PANEL = 256
ROWS = 4096
COLS = 384
CHUNK = 64
CHUNKS = COLS // CHUNK
WIDE = 128
SIDE = 4
CHIPS = 16

BLOCK = 168
S_ROW, OWN, FOREIGN = 128, 136, 152
STREAMS = ((0, 64, 32, 0), (64, 72, 40, 1), (OWN, 32, 32, 1))


def pick(index, values):
    result = jnp.int32(values[-1])
    for k in range(len(values) - 2, -1, -1):
        result = jnp.where(index == k, jnp.int32(values[k]), result)
    return result


def product(a, b, dims):
    return lax.dot_general(a, b, (dims, ((), ())), precision=HIGH, preferred_element_type=F32)


def dot(a, b):
    return product(a, b, ((1,), (0,)))


def dot_t(a, b):
    return product(a, b, ((0,), (0,)))


def dot_nt(a, b):
    return product(a, b, ((1,), (1,)))


def kernel(
    c_hbm, v_hbm, s_hbm, u_hbm, f_hbm, cbuf,
    buf, zacc, wacc, xa, xb, leads, wt, xfin, fac_u, fac_w,
    load_sem, c_sem, send_sem, side_sem, recv_sem, half_sem, sib_sem, uf_send, uf_recv, tail_recv, tail_sib,
    a_send, a_recv, b_send, b_recv, l_send, l_recv,
):
    z = lax.axis_index("row")
    col = lax.axis_index("col")
    core = lax.rem(col, 2)
    chip = lax.div(col, 2)
    x = lax.div(chip, SIDE)
    y = lax.rem(chip, SIDE)
    role = lax.rem(z, 4)
    group = lax.div(z, 4)
    sibling = col + 1 - 2 * core

    def chip_at(dx, dy):
        return lax.rem(x + dx, SIDE) * SIDE + lax.rem(y + dy, SIDE)

    def neighbour(axis, step):
        return chip_at(step, 0) * 2 + core if axis == 0 else chip_at(0, step) * 2 + core

    own_block = buf.at[chip, core]
    loads = [
        pltpu.make_async_copy(v_hbm, own_block.at[pl.ds(0, 128)], load_sem.at[0]),
        pltpu.make_async_copy(s_hbm, own_block.at[pl.ds(S_ROW, 8)], load_sem.at[1]),
        pltpu.make_async_copy(u_hbm, own_block.at[pl.ds(OWN, 8)], load_sem.at[2]),
        pltpu.make_async_copy(f_hbm, own_block.at[pl.ds(OWN + 8, 8)], load_sem.at[3]),
    ]
    for load in loads:
        load.start()
    load_c = pltpu.make_async_copy(c_hbm, cbuf, c_sem)
    load_c.start()

    barrier = pltpu.get_barrier_semaphore()
    for axis in (0, 1):
        for step in (1, 2, 3):
            pl.semaphore_signal(barrier, inc=1, device_id=(z, neighbour(axis, step)), device_id_type=MESH)
    pl.semaphore_signal(barrier, inc=1, device_id=(z, sibling), device_id_type=MESH)
    for step in range(1, 8):
        pl.semaphore_signal(barrier, inc=1, device_id=(lax.rem(z + step, 8), col), device_id_type=MESH)
    pl.semaphore_wait(barrier, 14)
    for load in loads:
        load.wait()

    def send(place, start, rows, to, sem):
        pltpu.make_async_remote_copy(
            src_ref=buf.at[place, core, pl.ds(start, rows)], dst_ref=buf.at[place, core, pl.ds(start, rows)],
            send_sem=send_sem, recv_sem=sem, device_id=(z, to), device_id_type=MESH,
        ).start()

    def to_sibling(place, start, rows, sem):
        pltpu.make_async_remote_copy(
            src_ref=buf.at[place, core, pl.ds(start, rows)], dst_ref=buf.at[place, core, pl.ds(start, rows)],
            send_sem=side_sem, recv_sem=sem, device_id=(z, sibling), device_id_type=MESH,
        ).start()

    def arrived(place, half, start, rows, sem):
        ref = buf.at[place, half, pl.ds(start, rows)]
        pltpu.make_async_copy(ref, ref, sem).wait()

    def index(axis, i, j):
        i, j = i % SIDE, j % SIDE
        return (i * SIDE + j) if axis == 0 else (j * SIDE + i)

    def place_of(h, i, j):
        return chip_at(i, j) if STREAMS[h][3] == 0 else chip_at(j, i)

    def first_axis(h):
        start, rows, _, axis = STREAMS[h]
        for step in (1, 3, 2):
            send(chip, start, rows, neighbour(axis, step), recv_sem.at[h, index(axis, -step, 0)])

    def second_axis(h, i):
        start, rows, _, axis = STREAMS[h]
        place = place_of(h, i, 0)
        if h == 2:
            for step in (1, 3, 2):
                send(place, start, rows, neighbour(1 - axis, step), tail_recv)
        else:
            for step in (1, 3):
                send(place, start, rows, neighbour(1 - axis, step), recv_sem.at[h, index(axis, i, -step)])

    def handle(h, i, j):
        start, rows, front, axis = STREAMS[h]
        place = place_of(h, i, j)
        here = index(axis, i, j)
        if j == 2:
            arrived(place, core, start, front, recv_sem.at[h, here])
            arrived(place, core, start + front, rows - front, half_sem.at[h, here])
        else:
            arrived(place, core, start, rows, recv_sem.at[h, here])
        if j == 0:
            second_axis(h, i)
        elif j == 3:
            send(place, start, front, neighbour(1 - axis, 1), recv_sem.at[h, index(axis, i, 2)])
        elif j == 1:
            send(place, start + front, rows - front, neighbour(1 - axis, 3), half_sem.at[h, index(axis, i, 2)])
        if h < 2:
            to_sibling(place, start, rows, sib_sem.at[h, here])

    def both(*offsets):
        for i, j in offsets:
            for h in (0, 1):
                handle(h, i, j)

    def vectors(q):
        return buf[q, :, pl.ds(0, 128), :].reshape(PANEL, PANEL)

    def project(*chips):
        @pl.loop(0, len(chips))
        def _(t):
            dx = pick(t, [c[0] for c in chips])
            dy = pick(t, [c[1] for c in chips])
            q = chip_at(dx, dy)
            for h in (0, 1):
                arrived(q, 1 - core, STREAMS[h][0], STREAMS[h][1], sib_sem.at[h, dx * SIDE + dy])
            rows = pl.ds(pl.multiple_of(q * 256, 256), 256)
            zacc[...] += dot_t(vectors(q), cbuf[rows, :])

    first_axis(0)
    first_axis(1)
    second_axis(0, 0)
    second_axis(1, 0)
    uf_to = pick(z, (3, 4, 1, 2, 0, 7, 5, 6))
    uf_copy = pltpu.make_async_remote_copy(
        src_ref=buf.at[chip, core, pl.ds(OWN, 16)], dst_ref=buf.at[chip, core, pl.ds(FOREIGN, 16)],
        send_sem=uf_send, recv_sem=uf_recv, device_id=(uf_to, col), device_id_type=MESH,
    )
    uf_copy.start()
    for h in (0, 1):
        to_sibling(chip, STREAMS[h][0], STREAMS[h][1], sib_sem.at[h, 0])
    zacc[...] = jnp.zeros_like(zacc)
    load_c.wait()
    both((1, 0), (3, 0))
    both((2, 0))
    uf_copy.wait()
    first_axis(2)
    both((0, 1), (0, 3))
    project((0, 0), (1, 0), (3, 0), (0, 1), (0, 3))
    both((1, 1), (1, 3), (3, 1), (3, 3))
    both((0, 2))
    second_axis(2, 0)
    project((2, 0), (0, 2))
    both((2, 1), (2, 3))
    for i in (1, 3, 2):
        handle(2, i, 0)
    project((1, 1), (1, 3), (3, 1), (3, 3))
    both((1, 2), (3, 2))
    both((2, 2))
    project((1, 2), (3, 2), (2, 1), (2, 3), (2, 2))

    def rows_of(c):
        return pl.ds(pl.multiple_of(c * CHUNK, CHUNK), CHUNK)

    def a_copy(c):
        to = jnp.where(role == 3, z - 1, z + 1)
        return pltpu.make_async_remote_copy(
            src_ref=xa.at[0, rows_of(c)], dst_ref=xa.at[1, rows_of(c)], send_sem=a_send.at[c],
            recv_sem=a_recv.at[c], device_id=(to, col), device_id_type=MESH,
        )

    def b_copy(c):
        to = jnp.where(role == 1, z + 1, z - 1)
        return pltpu.make_async_remote_copy(
            src_ref=xb.at[0, rows_of(c)], dst_ref=xb.at[1, rows_of(c)], send_sem=b_send.at[c],
            recv_sem=b_recv.at[c], device_id=(to, col), device_id_type=MESH,
        )

    def l_copy(c):
        to = jnp.where(role == 1, z - 1, lax.rem(z + 2, 8))
        return pltpu.make_async_remote_copy(
            src_ref=leads.at[2, rows_of(c)], dst_ref=leads.at[group, rows_of(c)], send_sem=l_send.at[c],
            recv_sem=l_recv.at[group, c], device_id=(to, col), device_id_type=MESH,
        )

    factor = buf[:, :, pl.ds(S_ROW, 8), :].reshape(PANEL, PANEL)
    head = vectors(jnp.int32(0))
    for c in range(COLS // WIDE):
        wide = slice(c * WIDE, (c + 1) * WIDE)
        w = dot_t(factor, zacc[:, wide])
        wacc[:, wide] = w
        xa[0, pl.ds(c * WIDE, WIDE), :] = (cbuf[pl.ds(0, PANEL), wide] - dot(head, w)).T

        @pl.when(role != 1)
        def _():
            for k in range(c * WIDE // CHUNK, (c + 1) * WIDE // CHUNK):
                a_copy(k).start()

    def lower(first, last):
        @pl.loop(first, last)
        def _(q):
            rows = pl.ds(pl.multiple_of(q * 256, 256), 256)
            cbuf[rows, :] = cbuf[rows, :] - dot(vectors(q), wacc[...])

    chain = (role == 1) | (role == 2)
    cut = jnp.where(chain, jnp.int32(4), jnp.int32(CHIPS))

    pltpu.make_async_copy(xa.at[0], xa.at[0], tail_recv).wait()
    tail = pltpu.make_async_remote_copy(
        src_ref=buf.at[:, core, pl.ds(OWN, 32)], dst_ref=buf.at[:, core, pl.ds(OWN, 32)],
        send_sem=side_sem, recv_sem=tail_sib, device_id=(z, sibling), device_id_type=MESH,
    )
    tail.start()
    lower(1, cut)
    tail.wait_recv()

    def prepare(slot, foreign):
        at = pl.multiple_of(jnp.where(foreign, jnp.int32(FOREIGN), jnp.int32(OWN)), 8)
        u = buf[:, :, pl.ds(at, 8), :].reshape(PANEL, PANEL)
        f = buf[:, :, pl.ds(at + 8, 8), :].reshape(PANEL, PANEL)
        fac_u[slot] = u
        fac_w[slot, pl.ds(0, PANEL), :] = f
        fac_w[slot, pl.ds(PANEL, PANEL), :] = dot(u, f)

    prepare(0, (role == 2) | (z == 0))
    prepare(1, role == 1)

    def weights(slot, leader, partner):
        return dot(jnp.concatenate([leader, partner], axis=1), fac_w[slot])

    a_lead = jnp.where(role == 2, jnp.int32(0), jnp.int32(1))
    b_lead = jnp.where(role == 1, jnp.int32(0), jnp.int32(1))

    @pl.when(role != 0)
    def _():
        @pl.loop(0, CHUNKS)
        def _(c):
            a_copy(c).wait_recv()
            leader = xa[a_lead, rows_of(c), :]
            w = weights(0, leader, xa[1 - a_lead, rows_of(c), :])
            wt[0, rows_of(c), :] = w
            xb[0, rows_of(c), :] = leader - w

            @pl.when(chain)
            def _():
                b_copy(c).start()

    @pl.when(chain)
    def _():
        @pl.loop(0, CHUNKS)
        def _(c):
            b_copy(c).wait_recv()
            leader = xb[b_lead, rows_of(c), :]
            w = weights(1, leader, xb[1 - b_lead, rows_of(c), :])
            wt[1, rows_of(c), :] = w
            leads[2, rows_of(c), :] = leader - w
            l_copy(c).start()

    @pl.when((role == 1) | (role == 3))
    def _():
        xfin[...] = xa[0] - dot_nt(wt[0], fac_u[0])

    @pl.when(role == 2)
    def _():
        xfin[...] = xb[0] - dot_nt(wt[1], fac_u[1])

    lower(cut, CHIPS)

    @pl.when(role == 0)
    def _():
        @pl.loop(0, CHUNKS)
        def _(c):
            for k in (0, 1):
                ref = leads.at[k, rows_of(c)]
                pltpu.make_async_copy(ref, ref, l_recv.at[k, c]).wait()
            leader, partner = leads[0, rows_of(c), :], leads[1, rows_of(c), :]
            w = weights(0, leader, partner)

            @pl.when(z == 0)
            def _():
                xfin[rows_of(c), :] = leader - w

            @pl.when(z != 0)
            def _():
                xfin[rows_of(c), :] = partner - dot_nt(w, fac_u[0])

    for c in range(COLS // WIDE):
        cbuf[pl.ds(0, PANEL), c * WIDE : (c + 1) * WIDE] = xfin[pl.ds(c * WIDE, WIDE), :].T

    sent = buf.at[pl.ds(0, CHIPS - 1), 0]
    pltpu.make_async_copy(sent, sent, send_sem).wait()
    sent = buf.at[:, 0]
    pltpu.make_async_copy(sent, sent, side_sem).wait()

    @pl.when(role != 1)
    def _():
        for c in range(CHUNKS):
            a_copy(c).wait_send()

    @pl.when(chain)
    def _():
        for c in range(CHUNKS):
            b_copy(c).wait_send()
            l_copy(c).wait_send()


def shards(trailing, leaf_vectors, leaf_factor, tree_vectors, tree_factor):
    dma = pltpu.SemaphoreType.DMA
    return pl.pallas_call(
        kernel,
        out_shape=pltpu.VMEM((ROWS, COLS), F32),
        in_specs=[pl.BlockSpec(memory_space=pltpu.HBM)] * 5,
        out_specs=pl.BlockSpec(memory_space=pltpu.VMEM),
        scratch_shapes=[
            pltpu.VMEM((CHIPS, 2, BLOCK, PANEL), F32),
            pltpu.VMEM((PANEL, COLS), F32),
            pltpu.VMEM((PANEL, COLS), F32),
            pltpu.VMEM((2, COLS, PANEL), F32),
            pltpu.VMEM((2, COLS, PANEL), F32),
            pltpu.VMEM((3, COLS, PANEL), F32),
            pltpu.VMEM((2, COLS, PANEL), F32),
            pltpu.VMEM((COLS, PANEL), F32),
            pltpu.VMEM((2, PANEL, PANEL), F32),
            pltpu.VMEM((2, 2 * PANEL, PANEL), F32),
            dma((4,)), dma, dma, dma, dma((3, CHIPS)), dma((2, CHIPS)), dma((2, CHIPS)), dma, dma, dma, dma,
            dma((CHUNKS,)), dma((CHUNKS,)), dma((CHUNKS,)), dma((CHUNKS,)), dma((CHUNKS,)), dma((2, CHUNKS)),
        ],
        compiler_params=pltpu.CompilerParams(
            collective_id=0, has_side_effects=True, vmem_limit_bytes=44 * 1024 * 1024
        ),
    )(trailing, leaf_vectors, leaf_factor, tree_vectors, tree_factor)


def solution(mesh):
    placed = (
        P("row", "col"),
        P(("row", "col"), None),
        P(("row", "col"), None),
        P(("row", "col"), None),
        P(("row", "col"), None),
    )
    return jax.shard_map(
        shards, mesh=mesh, in_specs=placed, out_specs=P("row", "col"), check_vma=False
    )
```

```python
import jax
import jax.numpy as jnp
from jax import lax
from jax.experimental import pallas as pl
from jax.experimental.pallas import tpu as pltpu
from jax.sharding import PartitionSpec as P

MESH = pl.DeviceIdType.MESH
HIGH = lax.Precision.HIGH
F32 = jnp.float32
BF16 = jnp.bfloat16

PANEL = 256
ROWS = 4096
COLS = 384
CHUNK = 64
CHUNKS = COLS // CHUNK
WIDE = 128
LAG = 3
SIDE = 4
CHIPS = 16

BLOCK = 168
S_ROW, OWN, FOREIGN = 128, 136, 152
STREAMS = ((0, 64, 32, 0), (64, 72, 40, 1), (OWN, 16, 16, 0), (FOREIGN, 16, 16, 1))


def pick(index, values):
    result = jnp.int32(values[-1])
    for k in range(len(values) - 2, -1, -1):
        result = jnp.where(index == k, jnp.int32(values[k]), result)
    return result


def product(a, b, dims):
    return lax.dot_general(a, b, (dims, ((), ())), precision=HIGH, preferred_element_type=F32)


def dot(a, b):
    return product(a, b, ((1,), (0,)))


def dot_t(a, b):
    return product(a, b, ((0,), (0,)))


def dot_nt(a, b):
    return product(a, b, ((1,), (1,)))


def kernel(
    c_hbm, v_hbm, s_hbm, u_hbm, f_hbm, cbuf,
    buf, zacc, wacc, xa, xb, leads, wt, xfin, fac_u, fac_high, fac_low,
    load_sem, c_sem, send_sem, side_sem, recv_sem, half_sem, sib_sem, uf_send, uf_recv, tail_recv, tail_sib,
    a_send, a_recv, b_send, b_recv, l_send, l_recv,
):
    z = lax.axis_index("row")
    col = lax.axis_index("col")
    core = lax.rem(col, 2)
    chip = lax.div(col, 2)
    x = lax.div(chip, SIDE)
    y = lax.rem(chip, SIDE)
    role = lax.rem(z, 4)
    group = lax.div(z, 4)
    sibling = col + 1 - 2 * core

    def chip_at(dx, dy):
        return lax.rem(x + dx, SIDE) * SIDE + lax.rem(y + dy, SIDE)

    def neighbour(axis, step):
        return chip_at(step, 0) * 2 + core if axis == 0 else chip_at(0, step) * 2 + core

    own_block = buf.at[chip, core]
    loads = [
        pltpu.make_async_copy(v_hbm, own_block.at[pl.ds(0, 128)], load_sem.at[0]),
        pltpu.make_async_copy(s_hbm, own_block.at[pl.ds(S_ROW, 8)], load_sem.at[1]),
        pltpu.make_async_copy(u_hbm, own_block.at[pl.ds(OWN, 8)], load_sem.at[2]),
        pltpu.make_async_copy(f_hbm, own_block.at[pl.ds(OWN + 8, 8)], load_sem.at[3]),
    ]
    for load in loads:
        load.start()
    load_c = pltpu.make_async_copy(c_hbm, cbuf, c_sem)
    load_c.start()

    barrier = pltpu.get_barrier_semaphore()
    for axis in (0, 1):
        for step in (1, 2, 3):
            pl.semaphore_signal(barrier, inc=1, device_id=(z, neighbour(axis, step)), device_id_type=MESH)
    pl.semaphore_signal(barrier, inc=1, device_id=(z, sibling), device_id_type=MESH)
    for step in range(1, 8):
        pl.semaphore_signal(barrier, inc=1, device_id=(lax.rem(z + step, 8), col), device_id_type=MESH)
    pl.semaphore_wait(barrier, 14)
    for load in loads:
        load.wait()

    def send(place, start, rows, to, sem):
        pltpu.make_async_remote_copy(
            src_ref=buf.at[place, core, pl.ds(start, rows)], dst_ref=buf.at[place, core, pl.ds(start, rows)],
            send_sem=send_sem, recv_sem=sem, device_id=(z, to), device_id_type=MESH,
        ).start()

    def to_sibling(place, start, rows, sem):
        pltpu.make_async_remote_copy(
            src_ref=buf.at[place, core, pl.ds(start, rows)], dst_ref=buf.at[place, core, pl.ds(start, rows)],
            send_sem=side_sem, recv_sem=sem, device_id=(z, sibling), device_id_type=MESH,
        ).start()

    def arrived(place, half, start, rows, sem):
        ref = buf.at[place, half, pl.ds(start, rows)]
        pltpu.make_async_copy(ref, ref, sem).wait()

    def index(axis, i, j):
        i, j = i % SIDE, j % SIDE
        return (i * SIDE + j) if axis == 0 else (j * SIDE + i)

    def place_of(h, i, j):
        return chip_at(i, j) if STREAMS[h][3] == 0 else chip_at(j, i)

    def first_axis(h):
        start, rows, _, axis = STREAMS[h]
        for step in (1, 3, 2):
            send(chip, start, rows, neighbour(axis, step), recv_sem.at[h, index(axis, -step, 0)])

    def second_axis(h, i):
        start, rows, _, axis = STREAMS[h]
        place = place_of(h, i, 0)
        if h >= 2:
            for step in (1, 3, 2):
                send(place, start, rows, neighbour(1 - axis, step), tail_recv)
        else:
            for step in (1, 3, 2) if i == 2 else (1, 3):
                send(place, start, rows, neighbour(1 - axis, step), recv_sem.at[h, index(axis, i, -step)])

    def handle(h, i, j):
        start, rows, front, axis = STREAMS[h]
        place = place_of(h, i, j)
        here = index(axis, i, j)
        if j == 2 and i != 2:
            arrived(place, core, start, front, recv_sem.at[h, here])
            arrived(place, core, start + front, rows - front, half_sem.at[h, here])
        else:
            arrived(place, core, start, rows, recv_sem.at[h, here])
        if j == 0:
            second_axis(h, i)
        elif j == 3 and i != 2:
            send(place, start, front, neighbour(1 - axis, 1), recv_sem.at[h, index(axis, i, 2)])
        elif j == 1 and i != 2:
            send(place, start + front, rows - front, neighbour(1 - axis, 3), half_sem.at[h, index(axis, i, 2)])
        if h < 2:
            to_sibling(place, start, rows, sib_sem.at[h, here])

    def both(*offsets):
        for i, j in offsets:
            for h in (0, 1):
                handle(h, i, j)

    def vectors(q):
        return buf[q, :, pl.ds(0, 128), :].reshape(PANEL, PANEL)

    def project(*chips):
        @pl.loop(0, len(chips))
        def _(t):
            dx = pick(t, [c[0] for c in chips])
            dy = pick(t, [c[1] for c in chips])
            q = chip_at(dx, dy)
            for h in (0, 1):
                arrived(q, 1 - core, STREAMS[h][0], STREAMS[h][1], sib_sem.at[h, dx * SIDE + dy])
            rows = pl.ds(pl.multiple_of(q * 256, 256), 256)
            zacc[...] += dot_t(vectors(q), cbuf[rows, :])

    first_axis(0)
    first_axis(1)
    second_axis(0, 0)
    second_axis(1, 0)
    uf_to = pick(z, (3, 4, 1, 2, 0, 7, 5, 6))
    uf_copy = pltpu.make_async_remote_copy(
        src_ref=buf.at[chip, core, pl.ds(OWN, 16)], dst_ref=buf.at[chip, core, pl.ds(FOREIGN, 16)],
        send_sem=uf_send, recv_sem=uf_recv, device_id=(uf_to, col), device_id_type=MESH,
    )
    uf_copy.start()
    for h in (0, 1):
        to_sibling(chip, STREAMS[h][0], STREAMS[h][1], sib_sem.at[h, 0])
    zacc[...] = jnp.zeros_like(zacc)
    load_c.wait()
    both((1, 0), (3, 0))
    both((2, 0))
    both((0, 1), (0, 3))
    uf_copy.wait()
    first_axis(2)
    first_axis(3)
    project((0, 0), (1, 0), (3, 0), (0, 1), (0, 3))
    both((1, 1), (1, 3), (3, 1), (3, 3))
    both((0, 2))
    project((2, 0), (0, 2))
    both((2, 1), (2, 3))
    for h in (2, 3):
        second_axis(h, 0)
    for i in (1, 3, 2):
        handle(2, i, 0)
        handle(3, i, 0)
    project((1, 1), (1, 3), (3, 1), (3, 3))
    both((1, 2), (3, 2))
    both((2, 2))
    project((1, 2), (3, 2), (2, 1), (2, 3), (2, 2))

    def rows_of(c):
        return pl.ds(pl.multiple_of(c * CHUNK, CHUNK), CHUNK)

    def a_copy(c):
        to = jnp.where(role == 3, z - 1, z + 1)
        return pltpu.make_async_remote_copy(
            src_ref=xa.at[0, rows_of(c)], dst_ref=xa.at[1, rows_of(c)], send_sem=a_send.at[c],
            recv_sem=a_recv.at[c], device_id=(to, col), device_id_type=MESH,
        )

    def b_copy(c):
        to = jnp.where(role == 1, z + 1, z - 1)
        return pltpu.make_async_remote_copy(
            src_ref=xb.at[0, rows_of(c)], dst_ref=xb.at[1, rows_of(c)], send_sem=b_send.at[c],
            recv_sem=b_recv.at[c], device_id=(to, col), device_id_type=MESH,
        )

    def l_copy(c):
        to = jnp.where(role == 1, z - 1, lax.rem(z + 2, 8))
        return pltpu.make_async_remote_copy(
            src_ref=leads.at[2, rows_of(c)], dst_ref=leads.at[group, rows_of(c)], send_sem=l_send.at[c],
            recv_sem=l_recv.at[group, c], device_id=(to, col), device_id_type=MESH,
        )

    factor = buf[:, :, pl.ds(S_ROW, 8), :].reshape(PANEL, PANEL)
    head = vectors(jnp.int32(0))
    for c in range(COLS // WIDE):
        wide = slice(c * WIDE, (c + 1) * WIDE)
        w = dot_t(factor, zacc[:, wide])
        wacc[:, wide] = w
        xa[0, pl.ds(c * WIDE, WIDE), :] = (cbuf[pl.ds(0, PANEL), wide] - dot(head, w)).T

        @pl.when(role != 1)
        def _():
            for k in range(c * WIDE // CHUNK, (c + 1) * WIDE // CHUNK):
                a_copy(k).start()

    def lower(first, last):
        @pl.loop(first, last)
        def _(q):
            rows = pl.ds(pl.multiple_of(q * 256, 256), 256)
            cbuf[rows, :] = cbuf[rows, :] - dot(vectors(q), wacc[...])

    chain = (role == 1) | (role == 2)
    cut = jnp.where(chain, jnp.int32(4), jnp.int32(CHIPS))

    pltpu.make_async_copy(xa.at[0], xa.at[0], tail_recv).wait()
    tail = pltpu.make_async_remote_copy(
        src_ref=buf.at[:, core, pl.ds(OWN, 32)], dst_ref=buf.at[:, core, pl.ds(OWN, 32)],
        send_sem=side_sem, recv_sem=tail_sib, device_id=(z, sibling), device_id_type=MESH,
    )
    tail.start()
    lower(1, cut)
    tail.wait_recv()

    def store_factor(slot, start, value):
        high = value.astype(BF16)
        fac_high[slot, pl.ds(start, PANEL), :] = high
        fac_low[slot, pl.ds(start, PANEL), :] = (value - high.astype(F32)).astype(BF16)

    def prepare(slot, foreign, last):
        at = pl.multiple_of(jnp.where(foreign, jnp.int32(FOREIGN), jnp.int32(OWN)), 8)
        u = buf[:, :, pl.ds(at, 8), :].reshape(PANEL, PANEL)
        f = buf[:, :, pl.ds(at + 8, 8), :].reshape(PANEL, PANEL)
        fac_u[slot] = u
        uf = dot(u, f)
        if last is None:
            store_factor(slot, 0, f)
            store_factor(slot, PANEL, uf)
        else:

            @pl.when(jnp.logical_not(last))
            def _():
                store_factor(slot, 0, f)
                store_factor(slot, PANEL, uf)

            @pl.when(last)
            def _():
                store_factor(slot, 0, dot_nt(f, u))
                store_factor(slot, PANEL, dot_nt(uf, u))

    prepare(0, (role == 2) | (z == 0), z == 4)

    @pl.when(chain)
    def _():
        prepare(1, role == 1, None)

    def plain(a, b):
        return jnp.dot(a, b, preferred_element_type=F32)

    def weights(slot, leader, partner):
        count = leader.shape[0]
        both_rows = jnp.concatenate([leader, partner], axis=1)
        high = both_rows.astype(BF16)
        low = (both_rows - high.astype(F32)).astype(BF16)
        main = plain(jnp.concatenate([high, low], axis=0), fac_high[slot])
        return main[:count] + (main[count:] + plain(high, fac_low[slot]))

    a_lead = jnp.where(role == 2, jnp.int32(0), jnp.int32(1))
    b_lead = jnp.where(role == 1, jnp.int32(0), jnp.int32(1))

    def a_step(c):
        a_copy(c).wait_recv()
        leader = xa[a_lead, rows_of(c), :]
        w = weights(0, leader, xa[1 - a_lead, rows_of(c), :])
        wt[0, rows_of(c), :] = w
        return leader - w

    def b_step(c):
        b_copy(c).wait_recv()
        leader = xb[b_lead, rows_of(c), :]
        w = weights(1, leader, xb[1 - b_lead, rows_of(c), :])
        leads[2, rows_of(c), :] = leader - w
        l_copy(c).start()
        wt[1, rows_of(c), :] = w

    @pl.when(role == 3)
    def _():
        @pl.loop(0, CHUNKS)
        def _(c):
            a_step(c)

    @pl.when(chain)
    def _():
        @pl.loop(0, CHUNKS + LAG)
        def _(t):
            @pl.when(t < CHUNKS)
            def _():
                xb[0, rows_of(t), :] = a_step(t)
                b_copy(t).start()

            @pl.when(t >= LAG)
            def _():
                b_step(t - LAG)

    @pl.when((role == 1) | (role == 3))
    def _():
        xfin[...] = xa[0] - dot_nt(wt[0], fac_u[0])

    @pl.when(role == 2)
    def _():
        xfin[...] = xb[1 - b_lead] - dot_nt(wt[1], fac_u[1])

    lower(cut, CHIPS)

    def store_top(c, value):
        cbuf[pl.ds(0, PANEL), pl.ds(pl.multiple_of(c * WIDE, WIDE), WIDE)] = value.T

    @pl.when(role != 0)
    def _():
        for c in range(COLS // WIDE):
            store_top(c, xfin[pl.ds(c * WIDE, WIDE), :])

    @pl.when(role == 0)
    def _():
        @pl.loop(0, COLS // WIDE)
        def _(c):
            for k in (0, 1):
                for half in range(WIDE // CHUNK):
                    ref = leads.at[k, pl.ds(0, CHUNK)]
                    pltpu.make_async_copy(ref, ref, l_recv.at[k, c * (WIDE // CHUNK) + half]).wait()
            rows = pl.ds(pl.multiple_of(c * WIDE, WIDE), WIDE)
            w = weights(0, leads[0, rows, :], leads[1, rows, :])
            store_top(c, leads[group, rows, :] - w)

    sent = buf.at[pl.ds(0, CHIPS - 1), 0]
    pltpu.make_async_copy(sent, sent, send_sem).wait()
    sent = buf.at[:, 0]
    pltpu.make_async_copy(sent, sent, side_sem).wait()

    @pl.when(role != 1)
    def _():
        for c in range(CHUNKS):
            a_copy(c).wait_send()

    @pl.when(chain)
    def _():
        for c in range(CHUNKS):
            b_copy(c).wait_send()
            l_copy(c).wait_send()


def shards(trailing, leaf_vectors, leaf_factor, tree_vectors, tree_factor):
    dma = pltpu.SemaphoreType.DMA
    return pl.pallas_call(
        kernel,
        out_shape=pltpu.VMEM((ROWS, COLS), F32),
        in_specs=[pl.BlockSpec(memory_space=pltpu.HBM)] * 5,
        out_specs=pl.BlockSpec(memory_space=pltpu.VMEM),
        scratch_shapes=[
            pltpu.VMEM((CHIPS, 2, BLOCK, PANEL), F32),
            pltpu.VMEM((PANEL, COLS), F32),
            pltpu.VMEM((PANEL, COLS), F32),
            pltpu.VMEM((2, COLS, PANEL), F32),
            pltpu.VMEM((2, COLS, PANEL), F32),
            pltpu.VMEM((3, COLS, PANEL), F32),
            pltpu.VMEM((2, COLS, PANEL), F32),
            pltpu.VMEM((COLS, PANEL), F32),
            pltpu.VMEM((2, PANEL, PANEL), F32),
            pltpu.VMEM((2, 2 * PANEL, PANEL), BF16),
            pltpu.VMEM((2, 2 * PANEL, PANEL), BF16),
            dma((4,)), dma, dma, dma, dma((4, CHIPS)), dma((2, CHIPS)), dma((2, CHIPS)), dma, dma, dma, dma,
            dma((CHUNKS,)), dma((CHUNKS,)), dma((CHUNKS,)), dma((CHUNKS,)), dma((CHUNKS,)), dma((2, CHUNKS)),
        ],
        compiler_params=pltpu.CompilerParams(
            collective_id=0, has_side_effects=True, vmem_limit_bytes=57 * 1024 * 1024
        ),
    )(trailing, leaf_vectors, leaf_factor, tree_vectors, tree_factor)


def solution(mesh):
    placed = (
        P("row", "col"),
        P(("row", "col"), None),
        P(("row", "col"), None),
        P(("row", "col"), None),
        P(("row", "col"), None),
    )
    return jax.shard_map(
        shards, mesh=mesh, in_specs=placed, out_specs=P("row", "col"), check_vma=False
    )
```

```python
import jax
import jax.numpy as jnp
from jax import lax
from jax.experimental import pallas as pl
from jax.experimental.pallas import tpu as pltpu
from jax.sharding import PartitionSpec as P

MESH = pl.DeviceIdType.MESH
HIGH = lax.Precision.HIGH
F32 = jnp.float32
BF16 = jnp.bfloat16

PANEL = 256
ROWS = 4096
COLS = 384
CHUNK = 64
CHUNKS = COLS // CHUNK
WIDE = 128
LAG = 3
GROUP = 128
SIDE = 4
CHIPS = 16

BLOCK = 168
S_ROW, OWN, FOREIGN = 128, 136, 152
STREAMS = ((0, 64, 32, 0), (64, 72, 40, 1), (OWN, 16, 16, 0), (FOREIGN, 16, 16, 1))


def pick(index, values):
    result = jnp.int32(values[-1])
    for k in range(len(values) - 2, -1, -1):
        result = jnp.where(index == k, jnp.int32(values[k]), result)
    return result


def product(a, b, dims):
    return lax.dot_general(a, b, (dims, ((), ())), precision=HIGH, preferred_element_type=F32)


def dot(a, b):
    return product(a, b, ((1,), (0,)))


def dot_t(a, b):
    return product(a, b, ((0,), (0,)))


def dot_nt(a, b):
    return product(a, b, ((1,), (1,)))


def plain(a, b):
    return jnp.dot(a, b, preferred_element_type=F32)


def halves(value):
    high = value.astype(BF16)
    return high, (value - high.astype(F32)).astype(BF16)


def split_dot(a, b_high, b_low):
    count = a.shape[0]
    high, low = halves(a)
    main = plain(jnp.concatenate([high, low], axis=0), b_high)
    return main[:count] + (main[count:] + plain(high, b_low))


def kernel(
    c_hbm, v_hbm, s_hbm, u_hbm, f_hbm, cbuf,
    buf, zt, ct, w_high, w_low, xa, xb, leads, wt, xfin, fac_u, fac_high, fac_low,
    load_sem, c_sem, send_sem, side_sem, recv_sem, half_sem, sib_sem, uf_send, uf_recv, tail_recv, tail_sib,
    a_send, a_recv, b_send, b_recv, l_send, l_recv,
):
    z = lax.axis_index("row")
    col = lax.axis_index("col")
    core = lax.rem(col, 2)
    chip = lax.div(col, 2)
    x = lax.div(chip, SIDE)
    y = lax.rem(chip, SIDE)
    role = lax.rem(z, 4)
    group = lax.div(z, 4)
    sibling = col + 1 - 2 * core

    def chip_at(dx, dy):
        return lax.rem(x + dx, SIDE) * SIDE + lax.rem(y + dy, SIDE)

    def neighbour(axis, step):
        return chip_at(step, 0) * 2 + core if axis == 0 else chip_at(0, step) * 2 + core

    own_block = buf.at[chip, core]
    loads = [
        pltpu.make_async_copy(v_hbm, own_block.at[pl.ds(0, 128)], load_sem.at[0]),
        pltpu.make_async_copy(s_hbm, own_block.at[pl.ds(S_ROW, 8)], load_sem.at[1]),
        pltpu.make_async_copy(u_hbm, own_block.at[pl.ds(OWN, 8)], load_sem.at[2]),
        pltpu.make_async_copy(f_hbm, own_block.at[pl.ds(OWN + 8, 8)], load_sem.at[3]),
    ]
    for load in loads:
        load.start()
    load_c = pltpu.make_async_copy(c_hbm, cbuf, c_sem)
    load_c.start()

    barrier = pltpu.get_barrier_semaphore()
    for axis in (0, 1):
        for step in (1, 2, 3):
            pl.semaphore_signal(barrier, inc=1, device_id=(z, neighbour(axis, step)), device_id_type=MESH)
    pl.semaphore_signal(barrier, inc=1, device_id=(z, sibling), device_id_type=MESH)
    for step in range(1, 8):
        pl.semaphore_signal(barrier, inc=1, device_id=(lax.rem(z + step, 8), col), device_id_type=MESH)
    pl.semaphore_wait(barrier, 14)
    for load in loads:
        load.wait()

    def send(place, start, rows, to, sem):
        pltpu.make_async_remote_copy(
            src_ref=buf.at[place, core, pl.ds(start, rows)], dst_ref=buf.at[place, core, pl.ds(start, rows)],
            send_sem=send_sem, recv_sem=sem, device_id=(z, to), device_id_type=MESH,
        ).start()

    def to_sibling(place, start, rows, sem):
        pltpu.make_async_remote_copy(
            src_ref=buf.at[place, core, pl.ds(start, rows)], dst_ref=buf.at[place, core, pl.ds(start, rows)],
            send_sem=side_sem, recv_sem=sem, device_id=(z, sibling), device_id_type=MESH,
        ).start()

    def arrived(place, half, start, rows, sem):
        ref = buf.at[place, half, pl.ds(start, rows)]
        pltpu.make_async_copy(ref, ref, sem).wait()

    def index(axis, i, j):
        i, j = i % SIDE, j % SIDE
        return (i * SIDE + j) if axis == 0 else (j * SIDE + i)

    def place_of(h, i, j):
        return chip_at(i, j) if STREAMS[h][3] == 0 else chip_at(j, i)

    def first_axis(h):
        start, rows, _, axis = STREAMS[h]
        for step in (1, 3, 2):
            send(chip, start, rows, neighbour(axis, step), recv_sem.at[h, index(axis, -step, 0)])

    def second_axis(h, i):
        start, rows, _, axis = STREAMS[h]
        place = place_of(h, i, 0)
        if h >= 2:
            for step in (1, 3, 2):
                send(place, start, rows, neighbour(1 - axis, step), tail_recv)
        else:
            for step in (1, 3):
                send(place, start, rows, neighbour(1 - axis, step), recv_sem.at[h, index(axis, i, -step)])

    def handle(h, i, j):
        start, rows, front, axis = STREAMS[h]
        place = place_of(h, i, j)
        here = index(axis, i, j)
        if j == 2:
            arrived(place, core, start, front, recv_sem.at[h, here])
            arrived(place, core, start + front, rows - front, half_sem.at[h, here])
        else:
            arrived(place, core, start, rows, recv_sem.at[h, here])
        if j == 0:
            second_axis(h, i)
        elif j == 3:
            send(place, start, front, neighbour(1 - axis, 1), recv_sem.at[h, index(axis, i, 2)])
        elif j == 1:
            send(place, start + front, rows - front, neighbour(1 - axis, 3), half_sem.at[h, index(axis, i, 2)])
        if h < 2:
            to_sibling(place, start, rows, sib_sem.at[h, here])

    def both(*offsets):
        for i, j in offsets:
            for h in (0, 1):
                handle(h, i, j)

    def vectors(q):
        return buf[q, :, pl.ds(0, 128), :].reshape(PANEL, PANEL)

    def project(*chips):
        @pl.loop(0, len(chips))
        def _(t):
            dx = pick(t, [c[0] for c in chips])
            dy = pick(t, [c[1] for c in chips])
            q = chip_at(dx, dy)
            for h in (0, 1):
                arrived(q, 1 - core, STREAMS[h][0], STREAMS[h][1], sib_sem.at[h, dx * SIDE + dy])
            rows = pl.ds(pl.multiple_of(q * 256, 256), 256)
            zt[...] += dot_t(cbuf[rows, :], vectors(q))

    first_axis(0)
    first_axis(1)
    second_axis(0, 0)
    second_axis(1, 0)
    uf_to = pick(z, (3, 4, 1, 2, 0, 7, 5, 6))
    uf_copy = pltpu.make_async_remote_copy(
        src_ref=buf.at[chip, core, pl.ds(OWN, 16)], dst_ref=buf.at[chip, core, pl.ds(FOREIGN, 16)],
        send_sem=uf_send, recv_sem=uf_recv, device_id=(uf_to, col), device_id_type=MESH,
    )
    uf_copy.start()
    for h in (0, 1):
        to_sibling(chip, STREAMS[h][0], STREAMS[h][1], sib_sem.at[h, 0])
    zt[...] = jnp.zeros_like(zt)
    load_c.wait()
    ct[...] = cbuf[pl.ds(0, PANEL), :].T
    both((1, 0), (3, 0))
    both((2, 0))
    both((0, 1), (0, 3))
    uf_copy.wait()
    first_axis(2)
    first_axis(3)
    project((0, 0), (1, 0), (3, 0), (0, 1), (0, 3))
    both((1, 1), (1, 3), (3, 1), (3, 3))
    both((0, 2))
    project((2, 0), (0, 2))
    both((2, 1), (2, 3))
    for h in (2, 3):
        second_axis(h, 0)
    for i in (1, 3, 2):
        handle(2, i, 0)
        handle(3, i, 0)
    project((1, 1), (1, 3), (3, 1), (3, 3))
    both((1, 2), (3, 2))
    project((1, 2), (3, 2), (2, 1), (2, 3))
    both((2, 2))
    project((2, 2))

    def rows_of(c):
        return pl.ds(pl.multiple_of(c * CHUNK, CHUNK), CHUNK)

    def a_copy(c):
        to = jnp.where(role == 3, z - 1, z + 1)
        return pltpu.make_async_remote_copy(
            src_ref=xa.at[0, rows_of(c)], dst_ref=xa.at[1, rows_of(c)], send_sem=a_send.at[c],
            recv_sem=a_recv.at[c], device_id=(to, col), device_id_type=MESH,
        )

    def b_copy(c):
        to = jnp.where(role == 1, z + 1, z - 1)
        return pltpu.make_async_remote_copy(
            src_ref=xb.at[0, rows_of(c)], dst_ref=xb.at[1, rows_of(c)], send_sem=b_send.at[c],
            recv_sem=b_recv.at[c], device_id=(to, col), device_id_type=MESH,
        )

    def l_copy(c):
        to = jnp.where(role == 1, z - 1, lax.rem(z + 2, 8))
        return pltpu.make_async_remote_copy(
            src_ref=leads.at[2, rows_of(c)], dst_ref=leads.at[group, rows_of(c)], send_sem=l_send.at[c],
            recv_sem=l_recv.at[group, c], device_id=(to, col), device_id_type=MESH,
        )

    s_halves = halves(buf[:, :, pl.ds(S_ROW, 8), :].reshape(PANEL, PANEL))
    head_halves = halves(vectors(jnp.int32(0)).T)
    for g in range(COLS // GROUP):
        rows = pl.ds(g * GROUP, GROUP)
        w = split_dot(zt[rows, :], *s_halves)
        zt[rows, :] = w
        xa[0, rows, :] = ct[rows, :] - split_dot(w, *head_halves)

        @pl.when(role != 1)
        def _():
            for k in range(g * GROUP // CHUNK, (g + 1) * GROUP // CHUNK):
                a_copy(k).start()

    w_high[...], w_low[...] = halves(zt[...].T)

    def lower(first, last):
        @pl.loop(first, last)
        def _(q):
            rows = pl.ds(pl.multiple_of(q * 256, 256), 256)
            cbuf[rows, :] = cbuf[rows, :] - split_dot(vectors(q), w_high[...], w_low[...])

    chain = (role == 1) | (role == 2)
    cut = jnp.where(chain, jnp.int32(9), jnp.int32(CHIPS))

    pltpu.make_async_copy(xa.at[0], xa.at[0], tail_recv).wait()
    tail = pltpu.make_async_remote_copy(
        src_ref=buf.at[:, core, pl.ds(OWN, 32)], dst_ref=buf.at[:, core, pl.ds(OWN, 32)],
        send_sem=side_sem, recv_sem=tail_sib, device_id=(z, sibling), device_id_type=MESH,
    )
    tail.start()
    lower(1, cut)
    tail.wait_recv()

    def store_factor(slot, start, value):
        rows = pl.ds(start, PANEL)
        fac_high[slot, rows, :], fac_low[slot, rows, :] = halves(value)

    def prepare(slot, foreign, last):
        at = pl.multiple_of(jnp.where(foreign, jnp.int32(FOREIGN), jnp.int32(OWN)), 8)
        u = buf[:, :, pl.ds(at, 8), :].reshape(PANEL, PANEL)
        f = buf[:, :, pl.ds(at + 8, 8), :].reshape(PANEL, PANEL)
        fac_u[slot] = u
        uf = dot(u, f)
        if last is None:
            store_factor(slot, 0, f)
            store_factor(slot, PANEL, uf)
        else:

            @pl.when(jnp.logical_not(last))
            def _():
                store_factor(slot, 0, f)
                store_factor(slot, PANEL, uf)

            @pl.when(last)
            def _():
                store_factor(slot, 0, dot_nt(f, u))
                store_factor(slot, PANEL, dot_nt(uf, u))

    prepare(0, (role == 2) | (z == 0), z == 4)

    @pl.when(chain)
    def _():
        prepare(1, role == 1, None)

    def weights(slot, leader, partner):
        return split_dot(jnp.concatenate([leader, partner], axis=1), fac_high[slot], fac_low[slot])

    a_lead = jnp.where(role == 2, jnp.int32(0), jnp.int32(1))
    b_lead = jnp.where(role == 1, jnp.int32(0), jnp.int32(1))

    def a_step(c):
        a_copy(c).wait_recv()
        leader = xa[a_lead, rows_of(c), :]
        w = weights(0, leader, xa[1 - a_lead, rows_of(c), :])
        wt[0, rows_of(c), :] = w
        return leader - w

    def b_step(c):
        b_copy(c).wait_recv()
        leader = xb[b_lead, rows_of(c), :]
        w = weights(1, leader, xb[1 - b_lead, rows_of(c), :])
        leads[2, rows_of(c), :] = leader - w
        l_copy(c).start()
        wt[1, rows_of(c), :] = w

    @pl.when(role == 3)
    def _():
        @pl.loop(0, CHUNKS)
        def _(c):
            a_step(c)

    @pl.when(chain)
    def _():
        @pl.loop(0, CHUNKS + LAG)
        def _(t):
            @pl.when(t < CHUNKS)
            def _():
                xb[0, rows_of(t), :] = a_step(t)
                b_copy(t).start()

            @pl.when(t >= LAG)
            def _():
                b_step(t - LAG)

    @pl.when((role == 1) | (role == 3))
    def _():
        xfin[...] = xa[0] - dot_nt(wt[0], fac_u[0])

    @pl.when(role == 2)
    def _():
        xfin[...] = xb[1 - b_lead] - dot_nt(wt[1], fac_u[1])

    lower(cut, CHIPS)

    def store_top(c, value):
        cbuf[pl.ds(0, PANEL), pl.ds(pl.multiple_of(c * WIDE, WIDE), WIDE)] = value.T

    @pl.when(role != 0)
    def _():
        for c in range(COLS // WIDE):
            store_top(c, xfin[pl.ds(c * WIDE, WIDE), :])

    @pl.when(role == 0)
    def _():
        done = 0
        for c in range(CHUNKS):
            for k in (0, 1):
                ref = leads.at[k, rows_of(c)]
                pltpu.make_async_copy(ref, ref, l_recv.at[k, c]).wait()
            w = weights(0, leads[0, rows_of(c), :], leads[1, rows_of(c), :])
            xfin[rows_of(c), :] = leads[group, rows_of(c), :] - w
            while (done + 1) * WIDE <= (c + 1) * CHUNK:
                store_top(done, xfin[pl.ds(done * WIDE, WIDE), :])
                done += 1

    sent = buf.at[pl.ds(0, CHIPS - 1), 0]
    pltpu.make_async_copy(sent, sent, send_sem).wait()
    sent = buf.at[:, 0]
    pltpu.make_async_copy(sent, sent, side_sem).wait()

    @pl.when(role != 1)
    def _():
        for c in range(CHUNKS):
            a_copy(c).wait_send()

    @pl.when(chain)
    def _():
        for c in range(CHUNKS):
            b_copy(c).wait_send()
            l_copy(c).wait_send()


def shards(trailing, leaf_vectors, leaf_factor, tree_vectors, tree_factor):
    dma = pltpu.SemaphoreType.DMA
    return pl.pallas_call(
        kernel,
        out_shape=pltpu.VMEM((ROWS, COLS), F32),
        in_specs=[pl.BlockSpec(memory_space=pltpu.HBM)] * 5,
        out_specs=pl.BlockSpec(memory_space=pltpu.VMEM),
        scratch_shapes=[
            pltpu.VMEM((CHIPS, 2, BLOCK, PANEL), F32),
            pltpu.VMEM((COLS, PANEL), F32),
            pltpu.VMEM((COLS, PANEL), F32),
            pltpu.VMEM((PANEL, COLS), BF16),
            pltpu.VMEM((PANEL, COLS), BF16),
            pltpu.VMEM((2, COLS, PANEL), F32),
            pltpu.VMEM((2, COLS, PANEL), F32),
            pltpu.VMEM((3, COLS, PANEL), F32),
            pltpu.VMEM((2, COLS, PANEL), F32),
            pltpu.VMEM((COLS, PANEL), F32),
            pltpu.VMEM((2, PANEL, PANEL), F32),
            pltpu.VMEM((2, 2 * PANEL, PANEL), BF16),
            pltpu.VMEM((2, 2 * PANEL, PANEL), BF16),
            dma((4,)), dma, dma, dma, dma((4, CHIPS)), dma((2, CHIPS)), dma((2, CHIPS)), dma, dma, dma, dma,
            dma((CHUNKS,)), dma((CHUNKS,)), dma((CHUNKS,)), dma((CHUNKS,)), dma((CHUNKS,)), dma((2, CHUNKS)),
        ],
        compiler_params=pltpu.CompilerParams(
            collective_id=0, has_side_effects=True, vmem_limit_bytes=57 * 1024 * 1024
        ),
    )(trailing, leaf_vectors, leaf_factor, tree_vectors, tree_factor)


def solution(mesh):
    placed = (
        P("row", "col"),
        P(("row", "col"), None),
        P(("row", "col"), None),
        P(("row", "col"), None),
        P(("row", "col"), None),
    )
    return jax.shard_map(
        shards, mesh=mesh, in_specs=placed, out_specs=P("row", "col"), check_vma=False
    )
```

```python
import jax
import jax.numpy as jnp
from jax import lax
from jax.experimental import pallas as pl
from jax.experimental.pallas import tpu as pltpu
from jax.sharding import PartitionSpec as P

MESH = pl.DeviceIdType.MESH
HIGH = lax.Precision.HIGH
F32 = jnp.float32
BF16 = jnp.bfloat16

PANEL = 256
ROWS = 4096
COLS = 384
CHUNK = 64
CHUNKS = COLS // CHUNK
WIDE = 128
LAG = 3
GROUP = 64
SIDE = 4
CHIPS = 16

BLOCK = 168
S_ROW, OWN, FOREIGN = 128, 136, 152
STREAMS = ((0, 64, 32, 0), (64, 72, 40, 1), (OWN, 16, 16, 0), (FOREIGN, 16, 16, 1))


def pick(index, values):
    result = jnp.int32(values[-1])
    for k in range(len(values) - 2, -1, -1):
        result = jnp.where(index == k, jnp.int32(values[k]), result)
    return result


def product(a, b, dims):
    return lax.dot_general(a, b, (dims, ((), ())), precision=HIGH, preferred_element_type=F32)


def dot(a, b):
    return product(a, b, ((1,), (0,)))


def dot_t(a, b):
    return product(a, b, ((0,), (0,)))


def dot_nt(a, b):
    return product(a, b, ((1,), (1,)))


def plain(a, b):
    return jnp.dot(a, b, preferred_element_type=F32)


def halves(value):
    high = value.astype(BF16)
    return high, (value - high.astype(F32)).astype(BF16)


def split_dot(a, b_high, b_low):
    count = a.shape[0]
    high, low = halves(a)
    main = plain(jnp.concatenate([high, low], axis=0), b_high)
    return main[:count] + (main[count:] + plain(high, b_low))


def kernel(
    c_hbm, v_hbm, s_hbm, u_hbm, f_hbm, cbuf,
    buf, zt, ct, w_high, w_low, xa, xb, leads, wt, xfin, fac_u, fac_high, fac_low,
    load_sem, c_sem, send_sem, side_sem, recv_sem, half_sem, sib_sem, uf_send, uf_recv, tail_recv, tail_sib,
    a_send, a_recv, b_send, b_recv, l_send, l_recv,
):
    z = lax.axis_index("row")
    col = lax.axis_index("col")
    core = lax.rem(col, 2)
    chip = lax.div(col, 2)
    x = lax.div(chip, SIDE)
    y = lax.rem(chip, SIDE)
    role = lax.rem(z, 4)
    group = lax.div(z, 4)
    sibling = col + 1 - 2 * core

    def chip_at(dx, dy):
        return lax.rem(x + dx, SIDE) * SIDE + lax.rem(y + dy, SIDE)

    def neighbour(axis, step):
        return chip_at(step, 0) * 2 + core if axis == 0 else chip_at(0, step) * 2 + core

    own_block = buf.at[chip, core]
    loads = [
        pltpu.make_async_copy(v_hbm, own_block.at[pl.ds(0, 128)], load_sem.at[0]),
        pltpu.make_async_copy(s_hbm, own_block.at[pl.ds(S_ROW, 8)], load_sem.at[1]),
        pltpu.make_async_copy(u_hbm, own_block.at[pl.ds(OWN, 8)], load_sem.at[2]),
        pltpu.make_async_copy(f_hbm, own_block.at[pl.ds(OWN + 8, 8)], load_sem.at[3]),
    ]
    for load in loads:
        load.start()
    load_c = pltpu.make_async_copy(c_hbm, cbuf, c_sem)
    load_c.start()

    barrier = pltpu.get_barrier_semaphore()
    for axis in (0, 1):
        for step in (1, 2, 3):
            pl.semaphore_signal(barrier, inc=1, device_id=(z, neighbour(axis, step)), device_id_type=MESH)
    pl.semaphore_signal(barrier, inc=1, device_id=(z, sibling), device_id_type=MESH)
    for step in range(1, 8):
        pl.semaphore_signal(barrier, inc=1, device_id=(lax.rem(z + step, 8), col), device_id_type=MESH)
    pl.semaphore_wait(barrier, 14)
    for load in loads:
        load.wait()

    def send(place, start, rows, to, sem):
        pltpu.make_async_remote_copy(
            src_ref=buf.at[place, core, pl.ds(start, rows)], dst_ref=buf.at[place, core, pl.ds(start, rows)],
            send_sem=send_sem, recv_sem=sem, device_id=(z, to), device_id_type=MESH,
        ).start()

    def to_sibling(place, start, rows, sem):
        pltpu.make_async_remote_copy(
            src_ref=buf.at[place, core, pl.ds(start, rows)], dst_ref=buf.at[place, core, pl.ds(start, rows)],
            send_sem=side_sem, recv_sem=sem, device_id=(z, sibling), device_id_type=MESH,
        ).start()

    def arrived(place, half, start, rows, sem):
        ref = buf.at[place, half, pl.ds(start, rows)]
        pltpu.make_async_copy(ref, ref, sem).wait()

    def index(axis, i, j):
        i, j = i % SIDE, j % SIDE
        return (i * SIDE + j) if axis == 0 else (j * SIDE + i)

    def place_of(h, i, j):
        return chip_at(i, j) if STREAMS[h][3] == 0 else chip_at(j, i)

    def first_axis(h):
        start, rows, _, axis = STREAMS[h]
        for step in (1, 3, 2):
            send(chip, start, rows, neighbour(axis, step), recv_sem.at[h, index(axis, -step, 0)])

    def second_axis(h, i):
        start, rows, _, axis = STREAMS[h]
        place = place_of(h, i, 0)
        if h >= 2:
            for step in (1, 3, 2):
                send(place, start, rows, neighbour(1 - axis, step), tail_recv)
        else:
            for step in (1, 3):
                send(place, start, rows, neighbour(1 - axis, step), recv_sem.at[h, index(axis, i, -step)])

    def handle(h, i, j):
        start, rows, front, axis = STREAMS[h]
        place = place_of(h, i, j)
        here = index(axis, i, j)
        if j == 2:
            arrived(place, core, start, front, recv_sem.at[h, here])
            arrived(place, core, start + front, rows - front, half_sem.at[h, here])
        else:
            arrived(place, core, start, rows, recv_sem.at[h, here])
        if j == 0:
            second_axis(h, i)
        elif j == 3:
            send(place, start, front, neighbour(1 - axis, 1), recv_sem.at[h, index(axis, i, 2)])
        elif j == 1:
            send(place, start + front, rows - front, neighbour(1 - axis, 3), half_sem.at[h, index(axis, i, 2)])
        if h < 2:
            to_sibling(place, start, rows, sib_sem.at[h, here])

    def both(*offsets):
        for i, j in offsets:
            for h in (0, 1):
                handle(h, i, j)

    def vectors(q):
        return buf[q, :, pl.ds(0, 128), :].reshape(PANEL, PANEL)

    def project(*chips):
        @pl.loop(0, len(chips))
        def _(t):
            dx = pick(t, [c[0] for c in chips])
            dy = pick(t, [c[1] for c in chips])
            q = chip_at(dx, dy)
            for h in (0, 1):
                arrived(q, 1 - core, STREAMS[h][0], STREAMS[h][1], sib_sem.at[h, dx * SIDE + dy])
            rows = pl.ds(pl.multiple_of(q * 256, 256), 256)
            zt[...] += dot_t(cbuf[rows, :], vectors(q))

    first_axis(0)
    first_axis(1)
    second_axis(0, 0)
    second_axis(1, 0)
    uf_to = pick(z, (3, 4, 1, 2, 0, 7, 5, 6))
    uf_copy = pltpu.make_async_remote_copy(
        src_ref=buf.at[chip, core, pl.ds(OWN, 16)], dst_ref=buf.at[chip, core, pl.ds(FOREIGN, 16)],
        send_sem=uf_send, recv_sem=uf_recv, device_id=(uf_to, col), device_id_type=MESH,
    )
    uf_copy.start()
    for h in (0, 1):
        to_sibling(chip, STREAMS[h][0], STREAMS[h][1], sib_sem.at[h, 0])
    zt[...] = jnp.zeros_like(zt)
    load_c.wait()
    ct[...] = cbuf[pl.ds(0, PANEL), :].T
    both((1, 0), (3, 0))
    both((2, 0))
    both((0, 1), (0, 3))
    uf_copy.wait()
    first_axis(2)
    first_axis(3)
    project((0, 0), (1, 0), (3, 0), (0, 1), (0, 3))
    both((1, 1), (1, 3), (3, 1), (3, 3))
    both((0, 2))
    project((2, 0), (0, 2))
    both((2, 1), (2, 3))
    for h in (2, 3):
        second_axis(h, 0)
    for i in (1, 3, 2):
        handle(2, i, 0)
        handle(3, i, 0)
    project((1, 1), (1, 3), (3, 1), (3, 3))
    both((1, 2), (3, 2))
    project((1, 2), (3, 2), (2, 1), (2, 3))
    both((2, 2))
    project((2, 2))

    def rows_of(c):
        return pl.ds(pl.multiple_of(c * CHUNK, CHUNK), CHUNK)

    def a_copy(c):
        to = jnp.where(role == 3, z - 1, z + 1)
        return pltpu.make_async_remote_copy(
            src_ref=xa.at[0, rows_of(c)], dst_ref=xa.at[1, rows_of(c)], send_sem=a_send.at[c],
            recv_sem=a_recv.at[c], device_id=(to, col), device_id_type=MESH,
        )

    def b_copy(c):
        to = jnp.where(role == 1, z + 1, z - 1)
        return pltpu.make_async_remote_copy(
            src_ref=xb.at[0, rows_of(c)], dst_ref=xb.at[1, rows_of(c)], send_sem=b_send.at[c],
            recv_sem=b_recv.at[c], device_id=(to, col), device_id_type=MESH,
        )

    def l_copy(c):
        to = jnp.where(role == 1, z - 1, lax.rem(z + 2, 8))
        return pltpu.make_async_remote_copy(
            src_ref=leads.at[2, rows_of(c)], dst_ref=leads.at[group, rows_of(c)], send_sem=l_send.at[c],
            recv_sem=l_recv.at[group, c], device_id=(to, col), device_id_type=MESH,
        )

    s_halves = halves(buf[:, :, pl.ds(S_ROW, 8), :].reshape(PANEL, PANEL))
    head_halves = halves(vectors(jnp.int32(0)).T)
    for g in range(COLS // GROUP):
        rows = pl.ds(g * GROUP, GROUP)
        w = split_dot(zt[rows, :], *s_halves)
        zt[rows, :] = w
        xa[0, rows, :] = ct[rows, :] - split_dot(w, *head_halves)

        @pl.when(role != 1)
        def _():
            for k in range(g * GROUP // CHUNK, (g + 1) * GROUP // CHUNK):
                a_copy(k).start()

    def lower(first, last):
        @pl.loop(first, last)
        def _(q):
            rows = pl.ds(pl.multiple_of(q * 256, 256), 256)
            cbuf[rows, :] = cbuf[rows, :] - split_dot(vectors(q), w_high[...], w_low[...])

    chain = (role == 1) | (role == 2)
    cut = jnp.where(chain, jnp.int32(5), jnp.int32(CHIPS))

    pltpu.make_async_copy(xa.at[0], xa.at[0], tail_recv).wait()
    tail = pltpu.make_async_remote_copy(
        src_ref=buf.at[:, core, pl.ds(OWN, 32)], dst_ref=buf.at[:, core, pl.ds(OWN, 32)],
        send_sem=side_sem, recv_sem=tail_sib, device_id=(z, sibling), device_id_type=MESH,
    )
    tail.start()
    w_high[...], w_low[...] = halves(zt[...].T)
    lower(1, cut)
    tail.wait_recv()

    def store_factor(slot, start, value):
        rows = pl.ds(start, PANEL)
        fac_high[slot, rows, :], fac_low[slot, rows, :] = halves(value)

    def prepare(slot, foreign, last):
        at = pl.multiple_of(jnp.where(foreign, jnp.int32(FOREIGN), jnp.int32(OWN)), 8)
        u = buf[:, :, pl.ds(at, 8), :].reshape(PANEL, PANEL)
        f = buf[:, :, pl.ds(at + 8, 8), :].reshape(PANEL, PANEL)
        fac_u[slot] = u
        uf = dot(u, f)
        if last is None:
            store_factor(slot, 0, f)
            store_factor(slot, PANEL, uf)
        else:

            @pl.when(jnp.logical_not(last))
            def _():
                store_factor(slot, 0, f)
                store_factor(slot, PANEL, uf)

            @pl.when(last)
            def _():
                store_factor(slot, 0, dot_nt(f, u))
                store_factor(slot, PANEL, dot_nt(uf, u))

    prepare(0, (role == 2) | (z == 0), z == 4)

    def weights(slot, leader, partner):
        return split_dot(jnp.concatenate([leader, partner], axis=1), fac_high[slot], fac_low[slot])

    a_lead = jnp.where(role == 2, jnp.int32(0), jnp.int32(1))
    b_lead = jnp.where(role == 1, jnp.int32(0), jnp.int32(1))

    def a_step(c):
        a_copy(c).wait_recv()
        leader = xa[a_lead, rows_of(c), :]
        w = weights(0, leader, xa[1 - a_lead, rows_of(c), :])
        wt[0, rows_of(c), :] = w
        return leader - w

    def b_step(c):
        b_copy(c).wait_recv()
        leader = xb[b_lead, rows_of(c), :]
        w = weights(1, leader, xb[1 - b_lead, rows_of(c), :])
        leads[2, rows_of(c), :] = leader - w
        l_copy(c).start()
        wt[1, rows_of(c), :] = w

    @pl.when(role == 3)
    def _():
        @pl.loop(0, CHUNKS)
        def _(c):
            a_step(c)

    @pl.when(chain)
    def _():
        def forward(t):
            xb[0, rows_of(t), :] = a_step(t)
            b_copy(t).start()

        @pl.loop(0, LAG)
        def _(t):
            forward(t)

        prepare(1, role == 1, None)

        @pl.loop(LAG, CHUNKS + LAG)
        def _(t):
            @pl.when(t < CHUNKS)
            def _():
                forward(t)

            b_step(t - LAG)

    @pl.when((role == 1) | (role == 3))
    def _():
        xfin[...] = xa[0] - dot_nt(wt[0], fac_u[0])

    @pl.when(role == 2)
    def _():
        xfin[...] = xb[1 - b_lead] - dot_nt(wt[1], fac_u[1])

    lower(cut, CHIPS)

    def store_top(c, value):
        cbuf[pl.ds(0, PANEL), pl.ds(pl.multiple_of(c * WIDE, WIDE), WIDE)] = value.T

    @pl.when(role != 0)
    def _():
        for c in range(COLS // WIDE):
            store_top(c, xfin[pl.ds(c * WIDE, WIDE), :])

    @pl.when(role == 0)
    def _():
        done = 0
        for c in range(CHUNKS):
            for k in (0, 1):
                ref = leads.at[k, rows_of(c)]
                pltpu.make_async_copy(ref, ref, l_recv.at[k, c]).wait()
            w = weights(0, leads[0, rows_of(c), :], leads[1, rows_of(c), :])
            xfin[rows_of(c), :] = leads[group, rows_of(c), :] - w
            while (done + 1) * WIDE <= (c + 1) * CHUNK:
                store_top(done, xfin[pl.ds(done * WIDE, WIDE), :])
                done += 1

    sent = buf.at[pl.ds(0, CHIPS - 1), 0]
    pltpu.make_async_copy(sent, sent, send_sem).wait()
    sent = buf.at[:, 0]
    pltpu.make_async_copy(sent, sent, side_sem).wait()

    @pl.when(role != 1)
    def _():
        for c in range(CHUNKS):
            a_copy(c).wait_send()

    @pl.when(chain)
    def _():
        for c in range(CHUNKS):
            b_copy(c).wait_send()
            l_copy(c).wait_send()


def shards(trailing, leaf_vectors, leaf_factor, tree_vectors, tree_factor):
    dma = pltpu.SemaphoreType.DMA
    return pl.pallas_call(
        kernel,
        out_shape=pltpu.VMEM((ROWS, COLS), F32),
        in_specs=[pl.BlockSpec(memory_space=pltpu.HBM)] * 5,
        out_specs=pl.BlockSpec(memory_space=pltpu.VMEM),
        scratch_shapes=[
            pltpu.VMEM((CHIPS, 2, BLOCK, PANEL), F32),
            pltpu.VMEM((COLS, PANEL), F32),
            pltpu.VMEM((COLS, PANEL), F32),
            pltpu.VMEM((PANEL, COLS), BF16),
            pltpu.VMEM((PANEL, COLS), BF16),
            pltpu.VMEM((2, COLS, PANEL), F32),
            pltpu.VMEM((2, COLS, PANEL), F32),
            pltpu.VMEM((3, COLS, PANEL), F32),
            pltpu.VMEM((2, COLS, PANEL), F32),
            pltpu.VMEM((COLS, PANEL), F32),
            pltpu.VMEM((2, PANEL, PANEL), F32),
            pltpu.VMEM((2, 2 * PANEL, PANEL), BF16),
            pltpu.VMEM((2, 2 * PANEL, PANEL), BF16),
            dma((4,)), dma, dma, dma, dma((4, CHIPS)), dma((2, CHIPS)), dma((2, CHIPS)), dma, dma, dma, dma,
            dma((CHUNKS,)), dma((CHUNKS,)), dma((CHUNKS,)), dma((CHUNKS,)), dma((CHUNKS,)), dma((2, CHUNKS)),
        ],
        compiler_params=pltpu.CompilerParams(
            collective_id=0, has_side_effects=True, vmem_limit_bytes=57 * 1024 * 1024
        ),
    )(trailing, leaf_vectors, leaf_factor, tree_vectors, tree_factor)


def solution(mesh):
    placed = (
        P("row", "col"),
        P(("row", "col"), None),
        P(("row", "col"), None),
        P(("row", "col"), None),
        P(("row", "col"), None),
    )
    return jax.shard_map(
        shards, mesh=mesh, in_specs=placed, out_specs=P("row", "col"), check_vma=False
    )
```

```python
import jax
import jax.numpy as jnp
from jax import lax
from jax.experimental import pallas as pl
from jax.experimental.pallas import tpu as pltpu
from jax.sharding import PartitionSpec as P

MESH = pl.DeviceIdType.MESH
HIGH = lax.Precision.HIGH
F32 = jnp.float32
BF16 = jnp.bfloat16

PANEL = 256
ROWS = 4096
COLS = 384
CHUNK = 64
CHUNKS = COLS // CHUNK
WIDE = 128
LAG = 3
GROUP = 64
SIDE = 4
CHIPS = 16

BLOCK = 168
S_ROW, OWN, FOREIGN = 128, 136, 152
STREAMS = ((0, 64, 32, 0), (64, 72, 40, 1), (OWN, 16, 16, 0), (FOREIGN, 16, 16, 1))


def pick(index, values):
    result = jnp.int32(values[-1])
    for k in range(len(values) - 2, -1, -1):
        result = jnp.where(index == k, jnp.int32(values[k]), result)
    return result


def product(a, b, dims):
    return lax.dot_general(a, b, (dims, ((), ())), precision=HIGH, preferred_element_type=F32)


def dot(a, b):
    return product(a, b, ((1,), (0,)))


def dot_t(a, b):
    return product(a, b, ((0,), (0,)))


def dot_nt(a, b):
    return product(a, b, ((1,), (1,)))


def plain(a, b):
    return jnp.dot(a, b, preferred_element_type=F32)


def halves(value):
    high = value.astype(BF16)
    return high, (value - high.astype(F32)).astype(BF16)


def split_dot(a, b_high, b_low):
    count = a.shape[0]
    high, low = halves(a)
    main = plain(jnp.concatenate([high, low], axis=0), b_high)
    return main[:count] + (main[count:] + plain(high, b_low))


def kernel(
    c_hbm, v_hbm, s_hbm, u_hbm, f_hbm, cbuf,
    buf, zt, ct, w_high, w_low, xa, xb, leads, wt, xfin, fac_u, fac_high, fac_low,
    load_sem, c_sem, send_sem, side_sem, recv_sem, half_sem, sib_sem, uf_send, uf_recv, tail_recv, tail_sib,
    a_send, a_recv, b_send, b_recv, l_send, l_recv,
):
    z = lax.axis_index("row")
    col = lax.axis_index("col")
    core = lax.rem(col, 2)
    chip = lax.div(col, 2)
    x = lax.div(chip, SIDE)
    y = lax.rem(chip, SIDE)
    role = lax.rem(z, 4)
    group = lax.div(z, 4)
    sibling = col + 1 - 2 * core

    def chip_at(dx, dy):
        return lax.rem(x + dx, SIDE) * SIDE + lax.rem(y + dy, SIDE)

    def neighbour(axis, step):
        return chip_at(step, 0) * 2 + core if axis == 0 else chip_at(0, step) * 2 + core

    own_block = buf.at[chip, core]
    loads = [
        pltpu.make_async_copy(v_hbm, own_block.at[pl.ds(0, 128)], load_sem.at[0]),
        pltpu.make_async_copy(s_hbm, own_block.at[pl.ds(S_ROW, 8)], load_sem.at[1]),
        pltpu.make_async_copy(u_hbm, own_block.at[pl.ds(OWN, 8)], load_sem.at[2]),
        pltpu.make_async_copy(f_hbm, own_block.at[pl.ds(OWN + 8, 8)], load_sem.at[3]),
    ]
    for load in loads:
        load.start()
    load_c = pltpu.make_async_copy(c_hbm, cbuf, c_sem)
    load_c.start()

    barrier = pltpu.get_barrier_semaphore()
    for axis in (0, 1):
        for step in (1, 2, 3):
            pl.semaphore_signal(barrier, inc=1, device_id=(z, neighbour(axis, step)), device_id_type=MESH)
    pl.semaphore_signal(barrier, inc=1, device_id=(z, sibling), device_id_type=MESH)
    for step in range(1, 8):
        pl.semaphore_signal(barrier, inc=1, device_id=(lax.rem(z + step, 8), col), device_id_type=MESH)
    pl.semaphore_wait(barrier, 14)
    for load in loads:
        load.wait()

    def send(place, start, rows, to, sem):
        pltpu.make_async_remote_copy(
            src_ref=buf.at[place, core, pl.ds(start, rows)], dst_ref=buf.at[place, core, pl.ds(start, rows)],
            send_sem=send_sem, recv_sem=sem, device_id=(z, to), device_id_type=MESH,
        ).start()

    def to_sibling(place, start, rows, sem):
        pltpu.make_async_remote_copy(
            src_ref=buf.at[place, core, pl.ds(start, rows)], dst_ref=buf.at[place, core, pl.ds(start, rows)],
            send_sem=side_sem, recv_sem=sem, device_id=(z, sibling), device_id_type=MESH,
        ).start()

    def arrived(place, half, start, rows, sem):
        ref = buf.at[place, half, pl.ds(start, rows)]
        pltpu.make_async_copy(ref, ref, sem).wait()

    def index(axis, i, j):
        i, j = i % SIDE, j % SIDE
        return (i * SIDE + j) if axis == 0 else (j * SIDE + i)

    def place_of(h, i, j):
        return chip_at(i, j) if STREAMS[h][3] == 0 else chip_at(j, i)

    def first_axis(h):
        start, rows, _, axis = STREAMS[h]
        for step in (1, 3) if h < 2 else (1, 3, 2):
            send(chip, start, rows, neighbour(axis, step), recv_sem.at[h, index(axis, -step, 0)])

    def second_axis(h, i):
        start, rows, _, axis = STREAMS[h]
        place = place_of(h, i, 0)
        if h >= 2:
            for step in (1, 3, 2):
                send(place, start, rows, neighbour(1 - axis, step), tail_recv)
        else:
            for step in (1, 3):
                send(place, start, rows, neighbour(1 - axis, step), recv_sem.at[h, index(axis, i, -step)])

    def handle(h, i, j):
        start, rows, front, axis = STREAMS[h]
        place = place_of(h, i, j)
        here = index(axis, i, j)
        if j == 2 or (h < 2 and j == 0 and i == 2):
            arrived(place, core, start, front, recv_sem.at[h, here])
            arrived(place, core, start + front, rows - front, half_sem.at[h, here])
        else:
            arrived(place, core, start, rows, recv_sem.at[h, here])
        if j == 0:
            if h < 2 and i == 3:
                send(place, start, front, neighbour(axis, 1), recv_sem.at[h, index(axis, 2, 0)])
            if h < 2 and i == 1:
                send(place, start + front, rows - front, neighbour(axis, 3), half_sem.at[h, index(axis, 2, 0)])
            second_axis(h, i)
        elif j == 3:
            send(place, start, front, neighbour(1 - axis, 1), recv_sem.at[h, index(axis, i, 2)])
        elif j == 1:
            send(place, start + front, rows - front, neighbour(1 - axis, 3), half_sem.at[h, index(axis, i, 2)])
        if h < 2:
            to_sibling(place, start, rows, sib_sem.at[h, here])

    def both(*offsets):
        for i, j in offsets:
            for h in (0, 1):
                handle(h, i, j)

    def vectors(q):
        return buf[q, :, pl.ds(0, 128), :].reshape(PANEL, PANEL)

    def project(*chips):
        @pl.loop(0, len(chips))
        def _(t):
            dx = pick(t, [c[0] for c in chips])
            dy = pick(t, [c[1] for c in chips])
            q = chip_at(dx, dy)
            for h in (0, 1):
                arrived(q, 1 - core, STREAMS[h][0], STREAMS[h][1], sib_sem.at[h, dx * SIDE + dy])
            rows = pl.ds(pl.multiple_of(q * 256, 256), 256)
            zt[...] += dot_t(cbuf[rows, :], vectors(q))

    first_axis(0)
    first_axis(1)
    second_axis(0, 0)
    second_axis(1, 0)
    uf_to = pick(z, (3, 4, 1, 2, 0, 7, 5, 6))
    uf_copy = pltpu.make_async_remote_copy(
        src_ref=buf.at[chip, core, pl.ds(OWN, 16)], dst_ref=buf.at[chip, core, pl.ds(FOREIGN, 16)],
        send_sem=uf_send, recv_sem=uf_recv, device_id=(uf_to, col), device_id_type=MESH,
    )
    uf_copy.start()
    for h in (0, 1):
        to_sibling(chip, STREAMS[h][0], STREAMS[h][1], sib_sem.at[h, 0])
    zt[...] = jnp.zeros_like(zt)
    load_c.wait()
    ct[...] = cbuf[pl.ds(0, PANEL), :].T
    both((1, 0), (3, 0))
    both((0, 1), (0, 3))
    both((2, 0))
    uf_copy.wait()
    first_axis(2)
    first_axis(3)
    project((0, 0), (1, 0), (3, 0), (0, 1), (0, 3))
    both((1, 1), (1, 3), (3, 1), (3, 3))
    both((0, 2))
    project((2, 0), (0, 2))
    both((2, 1), (2, 3))
    for h in (2, 3):
        second_axis(h, 0)
    for i in (1, 3, 2):
        handle(2, i, 0)
        handle(3, i, 0)
    project((1, 1), (1, 3), (3, 1), (3, 3))
    both((1, 2), (3, 2))
    project((1, 2), (3, 2), (2, 1), (2, 3))
    both((2, 2))
    project((2, 2))

    def rows_of(c):
        return pl.ds(pl.multiple_of(c * CHUNK, CHUNK), CHUNK)

    def a_copy(c):
        to = jnp.where(role == 3, z - 1, z + 1)
        return pltpu.make_async_remote_copy(
            src_ref=xa.at[0, rows_of(c)], dst_ref=xa.at[1, rows_of(c)], send_sem=a_send.at[c],
            recv_sem=a_recv.at[c], device_id=(to, col), device_id_type=MESH,
        )

    def b_copy(c):
        to = jnp.where(role == 1, z + 1, z - 1)
        return pltpu.make_async_remote_copy(
            src_ref=xb.at[0, rows_of(c)], dst_ref=xb.at[1, rows_of(c)], send_sem=b_send.at[c],
            recv_sem=b_recv.at[c], device_id=(to, col), device_id_type=MESH,
        )

    def l_copy(c):
        to = jnp.where(role == 1, z - 1, lax.rem(z + 2, 8))
        return pltpu.make_async_remote_copy(
            src_ref=leads.at[2, rows_of(c)], dst_ref=leads.at[group, rows_of(c)], send_sem=l_send.at[c],
            recv_sem=l_recv.at[group, c], device_id=(to, col), device_id_type=MESH,
        )

    s_halves = halves(buf[:, :, pl.ds(S_ROW, 8), :].reshape(PANEL, PANEL))
    head_halves = halves(vectors(jnp.int32(0)).T)
    for g in range(COLS // GROUP):
        rows = pl.ds(g * GROUP, GROUP)
        w = split_dot(zt[rows, :], *s_halves)
        zt[rows, :] = w
        xa[0, rows, :] = ct[rows, :] - split_dot(w, *head_halves)

        @pl.when(role != 1)
        def _():
            for k in range(g * GROUP // CHUNK, (g + 1) * GROUP // CHUNK):
                a_copy(k).start()

    def lower(first, last):
        @pl.loop(first, last)
        def _(q):
            rows = pl.ds(pl.multiple_of(q * 256, 256), 256)
            cbuf[rows, :] = cbuf[rows, :] - split_dot(vectors(q), w_high[...], w_low[...])

    chain = (role == 1) | (role == 2)
    cut = jnp.where(chain, jnp.int32(5), jnp.int32(CHIPS))

    pltpu.make_async_copy(xa.at[0], xa.at[0], tail_recv).wait()
    tail = pltpu.make_async_remote_copy(
        src_ref=buf.at[:, core, pl.ds(OWN, 32)], dst_ref=buf.at[:, core, pl.ds(OWN, 32)],
        send_sem=side_sem, recv_sem=tail_sib, device_id=(z, sibling), device_id_type=MESH,
    )
    tail.start()
    w_high[...], w_low[...] = halves(zt[...].T)
    lower(1, cut)
    tail.wait_recv()

    def store_factor(slot, start, value):
        rows = pl.ds(start, PANEL)
        fac_high[slot, rows, :], fac_low[slot, rows, :] = halves(value)

    def prepare(slot, foreign, last):
        at = pl.multiple_of(jnp.where(foreign, jnp.int32(FOREIGN), jnp.int32(OWN)), 8)
        u = buf[:, :, pl.ds(at, 8), :].reshape(PANEL, PANEL)
        f = buf[:, :, pl.ds(at + 8, 8), :].reshape(PANEL, PANEL)
        fac_u[slot] = u
        uf = dot(u, f)
        if last is None:
            store_factor(slot, 0, f)
            store_factor(slot, PANEL, uf)
        else:

            @pl.when(jnp.logical_not(last))
            def _():
                store_factor(slot, 0, f)
                store_factor(slot, PANEL, uf)

            @pl.when(last)
            def _():
                store_factor(slot, 0, dot_nt(f, u))
                store_factor(slot, PANEL, dot_nt(uf, u))

    prepare(0, (role == 2) | (z == 0), z == 4)

    def weights(slot, leader, partner):
        return split_dot(jnp.concatenate([leader, partner], axis=1), fac_high[slot], fac_low[slot])

    a_lead = jnp.where(role == 2, jnp.int32(0), jnp.int32(1))
    b_lead = jnp.where(role == 1, jnp.int32(0), jnp.int32(1))

    def a_step(c):
        a_copy(c).wait_recv()
        leader = xa[a_lead, rows_of(c), :]
        w = weights(0, leader, xa[1 - a_lead, rows_of(c), :])
        wt[0, rows_of(c), :] = w
        return leader - w

    def b_step(c):
        b_copy(c).wait_recv()
        leader = xb[b_lead, rows_of(c), :]
        w = weights(1, leader, xb[1 - b_lead, rows_of(c), :])
        leads[2, rows_of(c), :] = leader - w
        l_copy(c).start()
        wt[1, rows_of(c), :] = w

    @pl.when(role == 3)
    def _():
        @pl.loop(0, CHUNKS)
        def _(c):
            a_step(c)

    @pl.when(chain)
    def _():
        def forward(t):
            xb[0, rows_of(t), :] = a_step(t)
            b_copy(t).start()

        @pl.loop(0, LAG)
        def _(t):
            forward(t)

        prepare(1, role == 1, None)

        @pl.loop(LAG, CHUNKS + LAG)
        def _(t):
            @pl.when(t < CHUNKS)
            def _():
                forward(t)

            b_step(t - LAG)

    @pl.when((role == 1) | (role == 3))
    def _():
        xfin[...] = xa[0] - dot_nt(wt[0], fac_u[0])

    @pl.when(role == 2)
    def _():
        xfin[...] = xb[1 - b_lead] - dot_nt(wt[1], fac_u[1])

    lower(cut, CHIPS)

    def store_top(c, value):
        cbuf[pl.ds(0, PANEL), pl.ds(pl.multiple_of(c * WIDE, WIDE), WIDE)] = value.T

    @pl.when(role != 0)
    def _():
        for c in range(COLS // WIDE):
            store_top(c, xfin[pl.ds(c * WIDE, WIDE), :])

    @pl.when(role == 0)
    def _():
        done = 0
        for c in range(CHUNKS):
            for k in (0, 1):
                ref = leads.at[k, rows_of(c)]
                pltpu.make_async_copy(ref, ref, l_recv.at[k, c]).wait()
            w = weights(0, leads[0, rows_of(c), :], leads[1, rows_of(c), :])
            xfin[rows_of(c), :] = leads[group, rows_of(c), :] - w
            while (done + 1) * WIDE <= (c + 1) * CHUNK:
                store_top(done, xfin[pl.ds(done * WIDE, WIDE), :])
                done += 1

    sent = buf.at[pl.ds(0, CHIPS - 1), 0]
    pltpu.make_async_copy(sent, sent, send_sem).wait()
    sent = buf.at[:, 0]
    pltpu.make_async_copy(sent, sent, side_sem).wait()

    @pl.when(role != 1)
    def _():
        for c in range(CHUNKS):
            a_copy(c).wait_send()

    @pl.when(chain)
    def _():
        for c in range(CHUNKS):
            b_copy(c).wait_send()
            l_copy(c).wait_send()


def shards(trailing, leaf_vectors, leaf_factor, tree_vectors, tree_factor):
    dma = pltpu.SemaphoreType.DMA
    return pl.pallas_call(
        kernel,
        out_shape=pltpu.VMEM((ROWS, COLS), F32),
        in_specs=[pl.BlockSpec(memory_space=pltpu.HBM)] * 5,
        out_specs=pl.BlockSpec(memory_space=pltpu.VMEM),
        scratch_shapes=[
            pltpu.VMEM((CHIPS, 2, BLOCK, PANEL), F32),
            pltpu.VMEM((COLS, PANEL), F32),
            pltpu.VMEM((COLS, PANEL), F32),
            pltpu.VMEM((PANEL, COLS), BF16),
            pltpu.VMEM((PANEL, COLS), BF16),
            pltpu.VMEM((2, COLS, PANEL), F32),
            pltpu.VMEM((2, COLS, PANEL), F32),
            pltpu.VMEM((3, COLS, PANEL), F32),
            pltpu.VMEM((2, COLS, PANEL), F32),
            pltpu.VMEM((COLS, PANEL), F32),
            pltpu.VMEM((2, PANEL, PANEL), F32),
            pltpu.VMEM((2, 2 * PANEL, PANEL), BF16),
            pltpu.VMEM((2, 2 * PANEL, PANEL), BF16),
            dma((4,)), dma, dma, dma, dma((4, CHIPS)), dma((2, CHIPS)), dma((2, CHIPS)), dma, dma, dma, dma,
            dma((CHUNKS,)), dma((CHUNKS,)), dma((CHUNKS,)), dma((CHUNKS,)), dma((CHUNKS,)), dma((2, CHUNKS)),
        ],
        compiler_params=pltpu.CompilerParams(
            collective_id=0, has_side_effects=True, vmem_limit_bytes=57 * 1024 * 1024
        ),
    )(trailing, leaf_vectors, leaf_factor, tree_vectors, tree_factor)


def solution(mesh):
    placed = (
        P("row", "col"),
        P(("row", "col"), None),
        P(("row", "col"), None),
        P(("row", "col"), None),
        P(("row", "col"), None),
    )
    return jax.shard_map(
        shards, mesh=mesh, in_specs=placed, out_specs=P("row", "col"), check_vma=False
    )
```
